32 devices in a mesh: ctx: 4 (over x, core), shard: 8 (over z, y).
Axes of the slice: x: 2, y: 2, z: 4, core: 2. Of those that a mesh axis runs over, the one named last changes fastest.
Arguments:
- tokens: bfloat16 [8, 1024, 2048], P('shard', 'ctx'), may hold values from -6 to 6
- target: bfloat16 [8, 1024, 2048], P('shard', 'ctx'), may hold values from -6 to 6
- routes: int32 [8, 1024, 6], P('shard', 'ctx'), may hold values from 0 to 15, all different within a row; in each aligned block of 256 rows (0 to 255, 256 to 511, ..., all dimensions but the last counted through in order) at most 128 rows name the same one
- attn_gain: bfloat16 [2048], P('shard'), may hold values from 0.5 to 1.5
- w_query: bfloat16 [2048, 3072], P('shard'), may hold values from -0.125 to 0.125
- w_latent_in: bfloat16 [2048, 576], P('shard'), may hold values from -0.125 to 0.125
- latent_gain: bfloat16 [512], P('shard'), may hold values from 0.5 to 1.5
- w_latent_out: bfloat16 [512, 4096], P('shard'), may hold values from -0.25 to 0.25
- w_attn_out: bfloat16 [2048, 2048], P('shard'), may hold values from -2 to 2
- ffn_gain: bfloat16 [2048], P('shard'), may hold values from 0.5 to 1.5
- w_router: bfloat16 [2048, 16], P('shard'), may hold values from -0.0625 to 0.0625
- shared_gate: bfloat16 [2048, 2816], P('shard'), may hold values from -0.125 to 0.125
- shared_up: bfloat16 [2048, 2816], P('shard'), may hold values from -0.125 to 0.125
- shared_down: bfloat16 [2816, 2048], P('shard'), may hold values from -0.109375 to 0.109375
- expert_gate: bfloat16 [32, 2048, 704], P(('ctx', 'shard')), may hold values from -0.125 to 0.125
- expert_up: bfloat16 [32, 2048, 704], P(('ctx', 'shard')), may hold values from -0.125 to 0.125
- expert_down: bfloat16 [32, 704, 2048], P(('ctx', 'shard')), may hold values from -1.25 to 1.25
Outputs:
- layer_out: bfloat16 [8, 1024, 2048], P('shard', 'ctx')
- loss: float32 [], replicated
- token_grad: float32 [8, 1024, 2048], P('shard', 'ctx')
- attn_gain_grad: float32 [2048], P(('ctx', 'shard'))
- query_grad: float32 [2048, 3072], P(('ctx', 'shard'))
- latent_in_grad: float32 [2048, 576], P(('ctx', 'shard'))
- latent_gain_grad: float32 [512], P(('ctx', 'shard'))
- latent_out_grad: float32 [512, 4096], P(('ctx', 'shard'))
- attn_out_grad: float32 [2048, 2048], P(('ctx', 'shard'))
- ffn_gain_grad: float32 [2048], P(('ctx', 'shard'))
- router_grad: float32 [2048, 16], P(('ctx', 'shard'))
- shared_gate_grad: float32 [2048, 2816], P(('ctx', 'shard'))
- shared_up_grad: float32 [2048, 2816], P(('ctx', 'shard'))
- shared_down_grad: float32 [2816, 2048], P(('ctx', 'shard'))
- expert_gate_grad: float32 [32, 2048, 704], P(('ctx', 'shard'))
- expert_up_grad: float32 [32, 2048, 704], P(('ctx', 'shard'))
- expert_down_grad: float32 [32, 704, 2048], P(('ctx', 'shard'))
The draws below stay inside these ranges and needn't reach their ends.
Inputs may be any that keep to these rules, and one draw needn't show every extreme that they name: `routes`: each token names 6 different experts; among the 256 tokens of one device no expert is named more than 128 times, a bound that some block reaches.
All inputs are finite; a program needn't handle non-finite values.
Results may differ from the reference program's by a relative error of at most 0.014.
Values may be sent and summed in bfloat16 or wider, within the bound.
No kernel may reach another device: no remote copies, remote signals or barrier semaphores. Data moves between devices by JAX's collectives and lax.ppermute only.
A program may use at most 448 MiB of HBM per device.

```python
import math
import jax
import jax.numpy as jnp
import numpy as np
from jax import lax

D = 2048
H = 16
DN = 128
DR = 64
DV = 128
LAT = 512
FE = 1408
TOP = 6
BLOCK = 256
SEQ = 1024
TOK_DEV = 256
SEQS = 8
TOKENS = 8192
EXPERTS = 16
HALF = 704
FS = 2816
CAP = 128


def level_of(key, shape, cuts, smallest, largest):
    def one(dim, shards_of):
        steps = jax.random.uniform(jax.random.fold_in(jax.random.fold_in(key, 6), dim), (shards_of,), jnp.float32, smallest / len(cuts), largest / len(cuts))
        return jnp.repeat(jnp.exp(steps), shape[dim] // shards_of).reshape((-1,) + (1,) * (len(shape) - dim - 1))

    factor_of = one(*cuts[0])
    for cut in cuts[1:]:
        factor_of = factor_of * one(*cut)
    return factor_of


def shared_out(rng, own, number, rows, amount, top, limit, slope):
    sequence = jax.random.permutation(rng, amount)
    packed, common = portions_of(amount, rows * top, limit, slope, True), portions_of(amount, rows * top, limit, slope, False)
    places = jnp.arange(amount)

    def named(lengths, rotation):
        used = int((lengths > 0).sum())
        fixed = max(1, used // 4)
        passed = fixed + (places - fixed + rotation * (used - fixed)) % max(1, amount - fixed)
        return jnp.zeros((amount,), jnp.int32).at[sequence[jnp.where(places < fixed, places, passed)]].set(jnp.asarray(lengths, jnp.int32))

    lengths = jnp.where(number % 4 == 0, named(packed, number // 4), named(common, number - number // 4 - 1))
    mixed = jax.random.permutation(jax.random.fold_in(own, 3), amount)
    donor, receiver = mixed[0:amount // 2 * 2:2], mixed[1:amount // 2 * 2:2]
    room = jnp.minimum(lengths[donor] - 1, limit - lengths[receiver]) // 2
    room = jnp.where((donor == sequence[0]) | (receiver == sequence[0]) | (lengths[receiver] == 0), 0, jnp.maximum(room, 0))
    passed = jax.random.randint(jax.random.fold_in(own, 4), (amount // 2,), 0, 1 << 20) % (room + 1)
    lengths = lengths.at[donor].add(-passed).at[receiver].add(passed)
    labels = jnp.searchsorted(jnp.cumsum(lengths), jnp.arange(rows * top), side="right").astype(jnp.int32)
    listing = labels.reshape(top, rows).T
    listing = listing[jax.random.permutation(jax.random.fold_in(own, 1), rows)]
    rotation = jax.random.randint(jax.random.fold_in(own, 2), (rows, 1), 0, top)
    return jnp.take_along_axis(listing, (jnp.arange(top)[None, :] + rotation) % top, axis=1)


def portions_of(amount, total, limit, skew, full):
    loads = [(1 << 20) // math.isqrt(grade ** skew) + 1 for grade in range(1, amount + 1)]
    largest = limit if full else min(limit, max(-(-total // amount), total * loads[0] // sum(loads)))
    least = 1 if total - largest >= amount - 1 else 0
    given, surplus = [largest] + [least] * (amount - 1), total - largest - least * (amount - 1)
    while surplus > 0:
        candidates = [i for i in range(1, amount) if given[i] < largest] or [i for i in range(1, amount) if given[i] < limit]
        pool, budget = sum([loads[i] for i in candidates]), surplus
        for i in candidates:
            addition = min(limit - given[i], max(1, budget * loads[i] // pool), surplus)
            given[i] = given[i] + addition
            surplus = surplus - addition
    return np.array(given)


def bell_draw(stream_key, extent, scale, most, pieces=(), held_as=jnp.bfloat16):
    loudness = level_of(stream_key, extent, pieces, -0.22, 0.18) if pieces else 1.0
    values = jax.random.normal(stream_key, extent, jnp.float32) * scale * loudness
    return jnp.minimum(jnp.maximum(values, -most), most).astype(held_as)


def setup_inputs(seed: int = 0) -> dict:
    arg_keys = jax.random.split(jax.random.key(seed), 18)
    tokens = bell_draw(arg_keys[0], (SEQS, SEQ, D), 1.0, 6.0, ((0, 8), (1, 4)))
    target = bell_draw(arg_keys[1], (SEQS, SEQ, D), 1.0, 6.0, ((0, 8), (1, 4)))
    routes_keys = jax.random.split(jax.random.fold_in(arg_keys[2], 1), SEQS * SEQ // TOK_DEV)
    routes_turns = jax.random.permutation(jax.random.fold_in(arg_keys[2], 3), SEQS * SEQ // TOK_DEV)
    routes = jax.vmap(lambda own, number: shared_out(jax.random.fold_in(arg_keys[2], 2), own, number, TOK_DEV, EXPERTS, TOP, CAP, 1))(routes_keys, routes_turns).reshape((SEQS, SEQ, TOP))
    attn_gain = jnp.clip(1.0 + 0.1 * jax.random.normal(arg_keys[3], (D,), jnp.float32), 0.5, 1.5).astype(jnp.bfloat16)
    w_query = bell_draw(arg_keys[4], (D, H * (DN + DR)), D ** -0.5, 0.125, ((0, 8),))
    w_latent_in = bell_draw(arg_keys[5], (D, LAT + DR), D ** -0.5, 0.125, ((0, 8),))
    latent_gain = jnp.clip(1.0 + 0.1 * jax.random.normal(arg_keys[6], (LAT,), jnp.float32), 0.5, 1.5).astype(jnp.bfloat16)
    w_latent_out = bell_draw(arg_keys[7], (LAT, H * (DN + DV)), LAT ** -0.5, 0.25, ((0, 8),))
    w_attn_out = bell_draw(arg_keys[8], (H * DV, D), (max(D // 256, 1)) ** -0.5, 2.0, ((0, 8),))
    ffn_gain = jnp.clip(1.0 + 0.1 * jax.random.normal(arg_keys[9], (D,), jnp.float32), 0.5, 1.5).astype(jnp.bfloat16)
    w_router = bell_draw(arg_keys[10], (D, EXPERTS), (4 * D) ** -0.5, 0.0625, ((0, 8),))
    shared_gate = bell_draw(arg_keys[11], (D, FS), D ** -0.5, 0.125, ((0, 8),))
    shared_up = bell_draw(arg_keys[12], (D, FS), D ** -0.5, 0.125, ((0, 8),))
    shared_down = bell_draw(arg_keys[13], (FS, D), FS ** -0.5, 0.109375, ((0, 8),))
    expert_gate = bell_draw(arg_keys[14], (2 * EXPERTS, D, HALF), D ** -0.5, 0.125, ((0, 32),))
    expert_up = bell_draw(arg_keys[15], (2 * EXPERTS, D, HALF), D ** -0.5, 0.125, ((0, 32),))
    expert_down = bell_draw(arg_keys[16], (2 * EXPERTS, HALF, D), (max(FE // 64, 1)) ** -0.5, 1.25, ((0, 32),))
    return {"tokens": tokens, "target": target, "routes": routes, "attn_gain": attn_gain, "w_query": w_query, "w_latent_in": w_latent_in, "latent_gain": latent_gain, "w_latent_out": w_latent_out, "w_attn_out": w_attn_out, "ffn_gain": ffn_gain, "w_router": w_router, "shared_gate": shared_gate, "shared_up": shared_up, "shared_down": shared_down, "expert_gate": expert_gate, "expert_up": expert_up, "expert_down": expert_down}


@jax.custom_vjp
def low(v):
    return lax.optimization_barrier(v.astype(jnp.bfloat16)).astype(jnp.float32)

@jax.custom_vjp
def low_back(v):
    return v

def low_keep(v):
    return (low(v), None)

def low_pass(kept, grad):
    return (grad,)

def back_keep(v):
    return (v, None)

def back_low(kept, grad):
    return (low(grad),)
low.defvjp(low_keep, low_pass)
low_back.defvjp(back_keep, back_low)
HIGH = lax.Precision.HIGHEST

def mat(left, right):
    return jnp.dot(left, right, precision=HIGH, preferred_element_type=jnp.float32)

def rms_norm(values, gain):
    return values * lax.rsqrt(lax.optimization_barrier(jnp.mean(values * values, axis=-1, keepdims=True)) + 1e-06) * gain

def tables(position, width):
    half = width // 2
    freqs = 10000.0 ** (-jnp.arange(half, dtype=jnp.float32) / half)
    angle = position.astype(jnp.float32)[:, None] * freqs[None, :]
    return (jnp.cos(angle), jnp.sin(angle))

def rotate(values, cosine, sine):
    half = values.shape[-1] // 2
    first = values[..., :half]
    second = values[..., half:]
    return jnp.concatenate([first * cosine - second * sine, second * cosine + first * sine], -1)

def attend(query_plain, query_rope, pairs, key_rope):
    keys = pairs[..., :DN]
    values = pairs[..., DN:]
    scores = (jnp.einsum('qhd,khd->hqk', query_plain, keys, precision=HIGH) + jnp.einsum('qhd,kd->hqk', query_rope, key_rope, precision=HIGH)) * (DN + DR) ** (-0.5)
    scores = low_back(scores)
    place = jnp.arange(SEQ)
    visible = place[None, :] // BLOCK <= place[:, None] // BLOCK
    scores = jnp.where(visible[None], scores, -1e+30)
    probs = low(jax.nn.softmax(scores, axis=-1))
    return jnp.einsum('hqk,khd->qhd', probs, values, precision=HIGH)

def route_experts(rows_in, router, expert_gate, expert_up, expert_down, choose):
    blocks = TOKENS // TOK_DEV
    flat = choose.reshape(blocks, TOK_DEV * TOP).astype(jnp.int32)
    hot = (flat[:, :, None] == jnp.arange(EXPERTS, dtype=jnp.int32)[None, None, :]).astype(jnp.int32)
    before = jnp.cumsum(hot, axis=1, dtype=jnp.int32) - hot
    slots = lax.optimization_barrier(jnp.sum(before * hot, axis=-1, dtype=jnp.int32))
    places = (slots + (jnp.arange(blocks, dtype=jnp.int32) * CAP)[:, None]).astype(jnp.int32)
    owners = (jnp.arange(TOKENS * TOP, dtype=jnp.int32) // TOP).astype(jnp.int32)
    table = jnp.full((EXPERTS, blocks * CAP), TOKENS, jnp.int32).at[flat.reshape(-1), places.reshape(-1)].set(owners)
    padded_rows = jnp.concatenate([rows_in, jnp.zeros((1, D), jnp.float32)], 0)
    padded_router = jnp.concatenate([router, jnp.zeros((1, EXPERTS), jnp.float32)], 0)
    gate_full = expert_gate.reshape(EXPERTS, 2, D, HALF).transpose(0, 2, 1, 3).reshape(EXPERTS, D, FE)
    up_full = expert_up.reshape(EXPERTS, 2, D, HALF).transpose(0, 2, 1, 3).reshape(EXPERTS, D, FE)
    down_full = expert_down.reshape(EXPERTS, FE, D)

    def step(total, item):
        picked, gate_w, up_w, down_w, column = item
        taken = padded_rows[picked]
        weight = padded_router[picked, column]
        gate_val = low_back(mat(taken, gate_w))
        up_val = low_back(mat(taken, up_w))
        produced = low_back(mat(low(jax.nn.silu(gate_val) * up_val), down_w))
        return (total.at[picked].add(weight[:, None] * produced), None)
    carried = lax.scan(jax.checkpoint(step), jnp.zeros((TOKENS + 1, D), jnp.float32), (table, gate_full, up_full, down_full, jnp.arange(EXPERTS, dtype=jnp.int32)))
    return carried[0][:TOKENS]

def forward(source, attn_gain, w_query, w_latent_in, latent_gain, w_latent_out, w_attn_out, ffn_gain, w_router, shared_gate, shared_up, shared_down, expert_gate, expert_up, expert_down, routes):
    cosine, sine = tables(jnp.arange(SEQ), DR)
    attn_in = low(rms_norm(source, attn_gain))
    query = low_back(mat(attn_in, w_query)).reshape(SEQS, SEQ, H, DN + DR)
    query_plain = low(query[..., :DN])
    query_rope = low(rotate(query[..., DN:], cosine[:, None, :], sine[:, None, :]))
    latent_raw = low_back(mat(attn_in, w_latent_in))
    latent = low(rms_norm(latent_raw[..., :LAT], latent_gain))
    key_rope = low(rotate(latent_raw[..., LAT:], cosine, sine))
    pairs = low(mat(latent, w_latent_out)).reshape(SEQS, SEQ, H, DN + DV)
    checked = jax.checkpoint(attend)
    heads = lax.map(lambda item: checked(item[0], item[1], item[2], item[3]), (query_plain, query_rope, pairs, key_rope))
    heads = low(low_back(heads.reshape(SEQS, SEQ, H * DV)))
    middle = source + low_back(mat(heads, w_attn_out))
    ffn_in = low(rms_norm(middle, ffn_gain))
    router = jax.nn.softmax(low_back(mat(ffn_in, w_router)), axis=-1)
    gate_val = low_back(mat(ffn_in, shared_gate))
    up_val = low_back(mat(ffn_in, shared_up))
    shared_branch = low_back(mat(low(jax.nn.silu(gate_val) * up_val), shared_down))
    routed = route_experts(ffn_in.reshape(TOKENS, D), router.reshape(TOKENS, EXPERTS), expert_gate, expert_up, expert_down, routes.reshape(TOKENS, TOP))
    return middle + shared_branch + routed.reshape(SEQS, SEQ, D)

def reference(tokens, target, routes, attn_gain, w_query, w_latent_in, latent_gain, w_latent_out, w_attn_out, ffn_gain, w_router, shared_gate, shared_up, shared_down, expert_gate, expert_up, expert_down):
    params = [item.astype(jnp.float32) for item in (attn_gain, w_query, w_latent_in, latent_gain, w_latent_out, w_attn_out, ffn_gain, w_router, shared_gate, shared_up, shared_down, expert_gate, expert_up, expert_down)]

    def run(source, p0, p1, p2, p3, p4, p5, p6, p7, p8, p9, p10, p11, p12, p13):
        return forward(source, p0, p1, p2, p3, p4, p5, p6, p7, p8, p9, p10, p11, p12, p13, routes)
    final, pullback = jax.vjp(run, tokens.astype(jnp.float32), params[0], params[1], params[2], params[3], params[4], params[5], params[6], params[7], params[8], params[9], params[10], params[11], params[12], params[13])
    error = final - target.astype(jnp.float32)
    grads = pullback(error)
    return (final.astype(jnp.bfloat16), jnp.mean(error * error), grads[0], grads[1], grads[2], grads[3], grads[4], grads[5], grads[6], grads[7], grads[8], grads[9], grads[10], grads[11], grads[12], grads[13], grads[14])
```

```python
import functools

import jax
import jax.numpy as jnp
from jax import lax
from jax.experimental import pallas as pl
from jax.experimental.pallas import tpu as pltpu
from jax.sharding import PartitionSpec as P

H = 16
DN = 128
DR = 64
DV = 128
LAT = 512
TOP = 6
BLOCK = 256
LANES = 128

epsilon = 1e-06
base_freq = 10000.0
f32 = jnp.float32
bf16 = jnp.bfloat16


def tables(position, width):
    half = width // 2
    freqs = base_freq ** (-jnp.arange(half, dtype=f32) / half)
    angle = position.astype(f32)[:, None] * freqs[None, :]
    return (jnp.cos(angle), jnp.sin(angle))


def rotate(values, cosine, sine):
    half = values.shape[-1] // 2
    first = values[..., :half]
    second = values[..., half:]
    return jnp.concatenate([first * cosine - second * sine, second * cosine + first * sine], -1)


def rotate_back(grads, cosine, sine):
    return rotate(grads, cosine, -sine)


def inverse_root(values):
    return lax.rsqrt(jnp.mean(values * values, axis=-1, keepdims=True) + epsilon)


def norm_back(values, factor, gain, grads):
    scaled = grads * gain
    d_values = factor * scaled - values * factor**3 * jnp.mean(
        values * scaled, axis=-1, keepdims=True
    )
    return (d_values, jnp.sum(grads * values * factor, axis=0))


def silu_parts(values):
    sigma = jax.nn.sigmoid(values)
    return (values * sigma, sigma * (1.0 + values * (1.0 - sigma)))


def mm(left, right):
    return jnp.dot(left, right, preferred_element_type=f32)


def mm_nt(left, right):
    return lax.dot_general(left, right, (((1,), (1,)), ((), ())), preferred_element_type=f32)


def mm_tn(left, right):
    return lax.dot_general(left, right, (((0,), (0,)), ((), ())), preferred_element_type=f32)


def core_swap(value):
    count = lax.axis_size("ctx")
    return lax.ppermute(value, "ctx", [(i, i ^ 1) for i in range(count)])


def x_shift(value):
    count = lax.axis_size("ctx")
    return lax.ppermute(value, "ctx", [(i, (i + 2) % count) for i in range(count)])


def half_swap(value):
    count = lax.axis_size("shard")
    return lax.ppermute(value, "shard", [(i, i ^ 1) for i in range(count)])


def q_shift(value):
    count = lax.axis_size("shard")
    return lax.ppermute(value, "shard", [(i, (i + 2) % count) for i in range(count)])


def ring_sum(terms, shift):
    if len(terms) == 1:
        return terms[0].astype(f32)
    total = terms[1]
    for term in list(terms[2:]) + [terms[0]]:
        total = shift(total.astype(bf16)).astype(f32) + term.astype(f32)
    return total


def gather_x(block):
    found = [block]
    for _ in range(lax.axis_size("ctx") // 2 - 1):
        found.append(x_shift(found[-1]))
    return [[item, core_swap(item)] for item in found]


def scatter_x(terms):
    pairs = [item[0].astype(f32) + core_swap(item[1].astype(bf16)).astype(f32) for item in terms]
    return ring_sum(pairs, x_shift)


def place_of(dx, dc):
    ctx = lax.axis_index("ctx")
    chips = lax.axis_size("ctx") // 2
    return ((ctx // 2 - dx + chips) % chips) * 2 + (ctx % 2 + dc) % 2


def gather_ctx(block):
    rows = block.shape[0]
    full = jnp.zeros((rows * lax.axis_size("ctx"),) + block.shape[1:], block.dtype)
    for dx, pair in enumerate(gather_x(block)):
        for dc, item in enumerate(pair):
            full = lax.dynamic_update_slice_in_dim(full, item, place_of(dx, dc) * rows, 0)
    return full


def scatter_ctx(full):
    count = lax.axis_size("ctx")
    rows = full.shape[0] // count
    terms = [
        [lax.dynamic_slice_in_dim(full, place_of(dx, dc) * rows, rows, 0) for dc in range(2)]
        for dx in range(count // 2)
    ]
    return scatter_x(terms)


def scatter_shard(full):
    count = lax.axis_size("shard")
    me = lax.axis_index("shard")
    ring = count // 2
    sums = []
    for dq in range(ring):
        base = ((me // 2 - dq + ring) % ring) * 2
        own = lax.dynamic_index_in_dim(full, base + me % 2, 0, False)
        other = lax.dynamic_index_in_dim(full, base + 1 - me % 2, 0, False)
        sums.append(own.astype(f32) + half_swap(other.astype(bf16)).astype(f32))
    return ring_sum(sums, q_shift)


def attn_parts(q_ref, r_ref, p_ref, k_ref, block, scale):
    size = (block + 1) * BLOCK
    at = pl.ds(block * BLOCK, BLOCK)
    query = q_ref[at, :]
    rope = r_ref[0, at, :]
    keys = p_ref[0:size, 0:DN]
    values = p_ref[0:size, DN : DN + DV]
    key_rope = k_ref[0:size, :]
    scores = (mm_nt(query, keys) + mm_nt(rope, key_rope)) * scale
    weights = jnp.exp(scores - jnp.max(scores, axis=-1, keepdims=True))
    probs = weights / jnp.sum(weights, axis=-1, keepdims=True)
    return query, rope, keys, values, key_rope, probs, size, at


def attn_fwd_kernel(scale, q_ref, r_ref, p_ref, k_ref, o_ref):
    for block in range(q_ref.shape[0] // BLOCK):
        _, _, _, values, _, probs, _, at = attn_parts(q_ref, r_ref, p_ref, k_ref, block, scale)
        o_ref[at, :] = mm(probs.astype(bf16), values).astype(bf16)


def attn_bwd_kernel(scale, q_ref, r_ref, p_ref, k_ref, g_ref, dq_ref, dr_ref, dp_ref, dk_ref, sum_ref):
    @pl.when(pl.program_id(0) == 0)
    def _():
        dk_ref[...] = jnp.zeros_like(dk_ref)

    sum_ref[...] = jnp.zeros_like(sum_ref)
    for block in range(q_ref.shape[0] // BLOCK):
        query, rope, keys, values, key_rope, probs, size, at = attn_parts(
            q_ref, r_ref, p_ref, k_ref, block, scale
        )
        grad = g_ref[at, :]
        low = probs.astype(bf16)
        d_probs = mm_nt(grad, values)
        d_scores = probs * (d_probs - jnp.sum(probs * d_probs, axis=-1, keepdims=True))
        d_scores = d_scores.astype(bf16)
        dq_ref[at, :] = (mm(d_scores, keys) * scale).astype(bf16)
        dr_ref[0, at, :] = mm(d_scores, key_rope) * scale
        sum_ref[0:size, 0:DN] += mm_tn(d_scores, query) * scale
        sum_ref[0:size, DN : DN + DV] += mm_tn(low, grad)
        dk_ref[0:size, :] += mm_tn(d_scores, rope) * scale
    dp_ref[...] = sum_ref[...].astype(bf16)


def attn_specs(seq):
    return [
        pl.BlockSpec((seq, DN), lambda i: (0, i)),
        pl.BlockSpec((1, seq, DR), lambda i: (i, 0, 0)),
        pl.BlockSpec((seq, DN + DV), lambda i: (0, i)),
        pl.BlockSpec((seq, DR), lambda i: (0, 0)),
    ]


def attend(query, rope, pairs, key_rope, scale):
    seq = query.shape[0]
    heads = rope.shape[0]
    return pl.pallas_call(
        functools.partial(attn_fwd_kernel, scale),
        grid=(heads,),
        in_specs=attn_specs(seq),
        out_specs=pl.BlockSpec((seq, DV), lambda i: (0, i)),
        out_shape=jax.ShapeDtypeStruct((seq, heads * DV), bf16),
        compiler_params=pltpu.CompilerParams(vmem_limit_bytes=40 * 1024 * 1024),
        name="attend",
    )(query, rope, pairs, key_rope)


def attend_back(query, rope, pairs, key_rope, grad, scale):
    seq = query.shape[0]
    heads = rope.shape[0]
    return pl.pallas_call(
        functools.partial(attn_bwd_kernel, scale),
        grid=(heads,),
        in_specs=attn_specs(seq) + [pl.BlockSpec((seq, DV), lambda i: (0, i))],
        out_specs=[
            pl.BlockSpec((seq, DN), lambda i: (0, i)),
            pl.BlockSpec((1, seq, DR), lambda i: (i, 0, 0)),
            pl.BlockSpec((seq, DN + DV), lambda i: (0, i)),
            pl.BlockSpec((seq, DR), lambda i: (0, 0)),
        ],
        out_shape=[
            jax.ShapeDtypeStruct((seq, heads * DN), bf16),
            jax.ShapeDtypeStruct((heads, seq, DR), f32),
            jax.ShapeDtypeStruct((seq, heads * (DN + DV)), bf16),
            jax.ShapeDtypeStruct((seq, DR), f32),
        ],
        scratch_shapes=[pltpu.VMEM((seq, DN + DV), f32)],
        compiler_params=pltpu.CompilerParams(vmem_limit_bytes=40 * 1024 * 1024),
        name="attend_back",
    )(query, rope, pairs, key_rope, grad)


def on_device(
    tokens,
    target,
    routes,
    attn_gain,
    w_query,
    w_latent_in,
    latent_gain,
    w_latent_out,
    w_attn_out,
    ffn_gain,
    w_router,
    shared_gate,
    shared_up,
    shared_down,
    expert_gate,
    expert_up,
    expert_down,
):
    rows = tokens.shape[1]
    width = tokens.shape[2]
    ctx_count = lax.axis_size("ctx")
    shard_count = lax.axis_size("shard")
    chips = ctx_count // 2
    ring = shard_count // 2
    experts = ctx_count * ring
    capacity = max(2, (rows * TOP * 4 + experts * 3 - 1) // (experts * 3))
    seq_len = rows * ctx_count
    own_heads = H // ctx_count
    scale = (DN + DR) ** (-0.5)
    ctx = lax.axis_index("ctx")
    shard = lax.axis_index("shard")
    expert = ctx * ring + shard // 2
    devices = ctx_count * shard_count
    piece = width // devices

    gates_w = [expert_gate[0], half_swap(expert_gate[0])]
    ups_w = [expert_up[0], half_swap(expert_up[0])]
    downs_w = [expert_down[0], half_swap(expert_down[0])]

    depth = w_query.shape[0]
    small = jnp.concatenate([attn_gain, ffn_gain, latent_gain, w_router.reshape(-1)])
    small = lax.all_gather(small, "shard", axis=0, tiled=False)
    gain_attn = small[:, :depth].reshape(width).astype(f32)
    gain_ffn = small[:, depth : 2 * depth].reshape(width).astype(f32)
    lat_rows = latent_gain.shape[0]
    gain_latent = small[:, 2 * depth : 2 * depth + lat_rows].reshape(LAT).astype(f32)
    router_proj = small[:, 2 * depth + lat_rows :].reshape(width, experts)

    own_query = lax.dynamic_slice_in_dim(
        w_query, ctx * own_heads * (DN + DR), own_heads * (DN + DR), 1
    ).reshape(depth, own_heads, DN + DR)
    plain_cols = own_heads * DN
    rope_cols = own_heads * DR
    packed = jnp.concatenate(
        [
            own_query[..., :DN].reshape(depth, plain_cols),
            own_query[..., DN:].reshape(depth, rope_cols),
            w_latent_in,
        ],
        1,
    )
    packed = lax.all_gather(packed, "shard", axis=0, tiled=True)
    plain_proj = packed[:, :plain_cols]
    rope_proj = packed[:, plain_cols : plain_cols + rope_cols]
    latent_down = packed[:, plain_cols + rope_cols :]
    own_pairs = own_heads * (DN + DV)
    latent_up = lax.all_gather(
        lax.dynamic_slice_in_dim(w_latent_out, ctx * own_pairs, own_pairs, 1),
        "shard",
        axis=0,
        tiled=True,
    )
    out_piece = 0.0
    for j in range(ctx_count):
        moves = []
        for t in range(shard_count):
            to = t * ctx_count + j
            base = (to // shard_count) * shard_count
            moves.append((base + t, to))
        out_piece = out_piece + lax.ppermute(
            w_attn_out[j * piece : (j + 1) * piece], ("ctx", "shard"), moves
        )
    out_proj = lax.all_gather(out_piece, "shard", axis=0, tiled=True)

    slice_rows = shared_down.shape[0] // ctx_count
    down_own = lax.dynamic_slice_in_dim(shared_down, ctx * slice_rows, slice_rows, 0)
    shared_down_w = jnp.concatenate([down_own, half_swap(down_own)], 0)
    both = jnp.stack([shared_gate, shared_up], 1).reshape(
        depth, 2, shard_count, ctx_count, slice_rows
    )
    both = lax.dynamic_index_in_dim(both, ctx, 3, False)
    both = both.transpose(2, 0, 1, 3).reshape(shard_count, depth, 2 * slice_rows)
    both = lax.all_to_all(both, "shard", split_axis=0, concat_axis=0, tiled=True)
    both = both.reshape(width, 2 * slice_rows)
    both_other = half_swap(both)
    shared_gate_w = jnp.concatenate([both[:, :slice_rows], both_other[:, :slice_rows]], 1)
    shared_up_w = jnp.concatenate([both[:, slice_rows:], both_other[:, slice_rows:]], 1)

    source = tokens[0].astype(f32)
    factor_attn = inverse_root(source)
    all_source = gather_ctx(tokens[0]).astype(f32)
    attn_in = (all_source * inverse_root(all_source) * gain_attn).astype(bf16)
    cosine, sine = tables(jnp.arange(seq_len), DR)
    query = mm(attn_in, plain_proj).astype(bf16)
    query_rope = jnp.einsum(
        "td,dhk->htk",
        attn_in,
        rope_proj.reshape(width, own_heads, DR),
        preferred_element_type=f32,
    )
    query_rope = rotate(query_rope, cosine, sine).astype(bf16)
    latent_raw = mm(attn_in, latent_down)
    latent_part = latent_raw[:, :LAT]
    latent = (latent_part * inverse_root(latent_part) * gain_latent).astype(bf16)
    key_rope = rotate(latent_raw[:, LAT:], cosine, sine).astype(bf16)
    pairs = mm(latent, latent_up).astype(bf16)
    heads = attend(query, query_rope, pairs, key_rope, scale)
    middle = source + scatter_ctx(mm(heads, out_proj).astype(bf16))

    factor_ffn = inverse_root(middle)
    ffn_in = (middle * factor_ffn * gain_ffn).astype(bf16)
    router = jax.nn.softmax(mm(ffn_in, router_proj), axis=-1)
    chosen_any = jnp.any(
        routes[0][:, :, None] == jnp.arange(experts, dtype=jnp.int32)[None, None, :], axis=1
    )
    weight = jnp.where(chosen_any, router, -1.0)
    weight_high = weight.astype(bf16)
    weight_low = (weight - weight_high.astype(f32)).astype(bf16)
    info = jnp.concatenate(
        [
            weight_high,
            weight_low,
            jnp.zeros((rows, max(0, LANES - 2 * experts)), bf16),
        ],
        1,
    )
    info_cols = info.shape[1]

    def spread(block):
        found = []
        for step in range(ring):
            if step:
                block = q_shift(block)
            pairs_of = gather_x(block)
            found.append(jnp.stack([item for pair in pairs_of for item in pair], 0))
        return found

    def unspread(chunks):
        sums = []
        for chunk in chunks:
            terms = [[chunk[2 * dx], chunk[2 * dx + 1]] for dx in range(chips)]
            sums.append(scatter_x(terms))
        return ring_sum(sums, q_shift)

    before = (jnp.arange(rows)[:, None] <= jnp.arange(rows)[None, :]).astype(bf16)
    column = jnp.arange(info_cols)
    is_high = column == expert
    is_low = column == experts + expert

    kept = []
    outs = []
    for chunk in spread(jnp.concatenate([ffn_in, info], 1)):
        rows_in = chunk[..., :width]
        weights = jnp.sum(
            jnp.where(is_high | is_low, chunk[..., width:].astype(f32), 0.0), axis=-1
        )
        chosen = weights >= 0.0
        slot = jnp.einsum(
            "bt,tu->bu", chosen.astype(bf16), before, preferred_element_type=f32
        ).astype(jnp.int32)
        pick = (
            chosen[:, None, :]
            & (slot[:, None, :] == 1 + jnp.arange(capacity, dtype=jnp.int32)[None, :, None])
        )
        weight_row = jnp.sum(jnp.where(pick, weights[:, None, :], 0.0), axis=-1).reshape(-1, 1)
        pick = pick.astype(bf16)
        taken = (
            jnp.einsum("bjt,btd->bjd", pick, rows_in, preferred_element_type=f32)
            .astype(bf16)
            .reshape(-1, width)
        )
        gate_vals = [mm(taken, w) for w in gates_w]
        up_vals = [mm(taken, w) for w in ups_w]
        hidden = [g * jax.nn.sigmoid(g) * u for g, u in zip(gate_vals, up_vals)]
        scaled = [(v * weight_row).astype(bf16) for v in hidden]
        made = sum(mm(v, w) for v, w in zip(scaled, downs_w)).astype(bf16)
        flat = rows_in.reshape(-1, width)
        shared_gate_val = mm(flat, shared_gate_w)
        shared_up_val = mm(flat, shared_up_w)
        shared_hidden = (
            shared_gate_val * jax.nn.sigmoid(shared_gate_val) * shared_up_val
        ).astype(bf16)
        out = jnp.einsum(
            "bjt,bjd->btd",
            pick,
            made.reshape(-1, capacity, width),
            preferred_element_type=f32,
        ) + mm(shared_hidden, shared_down_w).reshape(rows_in.shape)
        outs.append(out.astype(bf16))
        kept.append(
            (
                flat,
                pick,
                weight_row,
                taken,
                gate_vals,
                up_vals,
                scaled,
                shared_gate_val,
                shared_up_val,
                shared_hidden,
            )
        )
    final = middle + unspread(outs)
    error = final - target[0].astype(f32)
    loss_part = jnp.sum(error * error)

    d_chunks = []
    grads = []
    for chunk, saved in zip(spread(error.astype(bf16)), kept):
        (
            flat,
            pick,
            weight_row,
            taken,
            gate_vals,
            up_vals,
            scaled,
            shared_gate_val,
            shared_up_val,
            shared_hidden,
        ) = saved
        d_flat = chunk.reshape(-1, width)
        d_taken = (
            jnp.einsum("bjt,btd->bjd", pick, chunk, preferred_element_type=f32)
            .astype(bf16)
            .reshape(-1, width)
        )
        d_weight = 0.0
        d_gates = []
        d_ups = []
        for g, u, w in zip(gate_vals, up_vals, downs_w):
            act, slope = silu_parts(g)
            d_plain = mm_nt(d_taken, w)
            d_weight = d_weight + jnp.sum(
                (act * u).astype(bf16).astype(f32) * d_plain, axis=-1, keepdims=True
            )
            d_hidden = d_plain * weight_row
            d_gates.append((d_hidden * u * slope).astype(bf16))
            d_ups.append((d_hidden * act).astype(bf16))
        d_rows = sum(mm_nt(v, w) for v, w in zip(d_gates, gates_w)) + sum(
            mm_nt(v, w) for v, w in zip(d_ups, ups_w)
        )
        shared_act, shared_slope = silu_parts(shared_gate_val)
        d_shared_hidden = mm_nt(d_flat, shared_down_w)
        d_shared_gate = (d_shared_hidden * shared_up_val * shared_slope).astype(bf16)
        d_shared_up = (d_shared_hidden * shared_act).astype(bf16)
        d_block = jnp.einsum(
            "bjt,bjd->btd",
            pick,
            d_rows.astype(bf16).reshape(-1, capacity, width),
            preferred_element_type=f32,
        ) + (mm_nt(d_shared_gate, shared_gate_w) + mm_nt(d_shared_up, shared_up_w)).reshape(
            chunk.shape
        )
        d_weight = jnp.sum(
            jnp.where(pick > 0, d_weight.reshape(-1, capacity, 1), 0.0), axis=1
        )[..., None]
        d_high = d_weight.astype(bf16)
        d_low = (d_weight - d_high.astype(f32)).astype(bf16)
        zero = jnp.zeros((), bf16)
        d_info = jnp.where(is_high, d_high, jnp.where(is_low, d_low, zero))
        d_chunks.append(jnp.concatenate([d_block.astype(bf16), d_info], -1))
        grads.append(
            (
                taken,
                d_taken,
                scaled,
                d_gates,
                d_ups,
                mm_tn(shared_hidden, d_flat),
                mm_tn(flat, d_shared_gate),
                mm_tn(flat, d_shared_up),
            )
        )
    d_all = unspread(d_chunks)
    d_ffn = d_all[:, :width]
    d_info = d_all[:, width:]
    d_router = d_info[:, :experts] + d_info[:, experts : 2 * experts]
    d_router = jnp.where(chosen_any, d_router, 0.0)

    taken = jnp.concatenate([item[0] for item in grads], 0)
    d_taken = jnp.concatenate([item[1] for item in grads], 0)
    d_expert = []
    for half in (1, 0):
        scaled = jnp.concatenate([item[2][half] for item in grads], 0)
        d_gates = jnp.concatenate([item[3][half] for item in grads], 0)
        d_ups = jnp.concatenate([item[4][half] for item in grads], 0)
        d_expert.append((mm_tn(taken, d_gates), mm_tn(taken, d_ups), mm_tn(scaled, d_taken)))
    d_expert = [own + half_swap(other.astype(bf16)).astype(f32) for other, own in zip(*d_expert)]

    def halves(value, axis):
        own = lax.slice_in_dim(value, 0, slice_rows, axis=axis)
        other = lax.slice_in_dim(value, slice_rows, 2 * slice_rows, axis=axis)
        return own, other

    d_shared_down = sum(item[5] for item in grads)
    d_shared_gate = sum(item[6] for item in grads)
    d_shared_up = sum(item[7] for item in grads)
    own, other = halves(d_shared_down, 0)
    d_shared_down = own + half_swap(other.astype(bf16)).astype(f32)
    moves = []
    for a in range(ctx_count):
        for b in range(shard_count):
            moves.append((a * shard_count + b, b * ctx_count + a))
    g_down = lax.ppermute(d_shared_down.astype(bf16), ("ctx", "shard"), moves).astype(f32)
    gate_own, gate_other = halves(d_shared_gate, 1)
    up_own, up_other = halves(d_shared_up, 1)
    d_both = jnp.concatenate([gate_own, up_own], 1) + half_swap(
        jnp.concatenate([gate_other, up_other], 1).astype(bf16)
    ).astype(f32)
    d_both = lax.all_to_all(
        d_both.astype(bf16).reshape(devices, piece, 2 * slice_rows),
        ("ctx", "shard"),
        split_axis=0,
        concat_axis=0,
        tiled=True,
    )
    d_both = d_both.reshape(ctx_count, shard_count, piece, 2, slice_rows)
    d_both = d_both.transpose(3, 2, 1, 0, 4).reshape(2, piece, -1).astype(f32)
    g_gate = d_both[0]
    g_up = d_both[1]

    d_logits = (router * (d_router - jnp.sum(router * d_router, axis=-1, keepdims=True))).astype(
        bf16
    )
    d_router_proj = mm_tn(ffn_in, d_logits)
    d_ffn = d_ffn + mm_nt(d_logits, router_proj)
    d_middle_norm, d_gain_ffn = norm_back(middle, factor_ffn, gain_ffn, d_ffn)
    d_middle = error + d_middle_norm

    d_branch = gather_ctx(d_middle.astype(bf16))
    d_out_proj = mm_tn(heads, d_branch)
    g_attn_out = scatter_shard(d_out_proj.reshape(shard_count, piece, width))
    d_heads = mm_nt(d_branch, out_proj).astype(bf16)
    d_query, d_rope, d_pairs, d_key_rope = attend_back(
        query, query_rope, pairs, key_rope, d_heads, scale
    )
    d_rope = rotate_back(d_rope, cosine, sine).astype(bf16)
    d_rope = d_rope.transpose(1, 0, 2).reshape(seq_len, rope_cols)
    d_latent_up = mm_tn(latent, d_pairs)
    d_latent = scatter_ctx(jnp.concatenate([mm_nt(d_pairs, latent_up), d_key_rope], 1))
    first = ctx * rows
    own_latent = lax.dynamic_slice_in_dim(latent_part, first, rows, 0)
    d_latent_part, d_gain_latent = norm_back(
        own_latent, inverse_root(own_latent), gain_latent, d_latent[:, :LAT]
    )
    own_cosine = lax.dynamic_slice_in_dim(cosine, first, rows, 0)
    own_sine = lax.dynamic_slice_in_dim(sine, first, rows, 0)
    d_latent_raw = jnp.concatenate(
        [d_latent_part, rotate_back(d_latent[:, LAT:], own_cosine, own_sine)], -1
    ).astype(bf16)
    latent_cols = (LAT + DR) // ctx_count
    d_latent_all = lax.dynamic_slice_in_dim(
        gather_ctx(d_latent_raw), ctx * latent_cols, latent_cols, 1
    )
    d_packed = mm_tn(attn_in, jnp.concatenate([d_query, d_rope, d_latent_all], 1)).astype(bf16)
    d_attn_in = scatter_ctx(
        (mm_nt(d_query, plain_proj) + mm_nt(d_rope, rope_proj)).astype(bf16)
    ) + mm_nt(d_latent_raw, latent_down)
    d_source_norm, d_gain_attn = norm_back(source, factor_attn, gain_attn, d_attn_in)
    token_grad = d_middle + d_source_norm

    def to_rows(value):
        cols = value.shape[1]
        value = value.reshape(ctx_count, shard_count, -1, cols).transpose(1, 0, 2, 3)
        value = scatter_shard(value).astype(bf16)
        return lax.all_to_all(value, "ctx", split_axis=0, concat_axis=0, tiled=True).astype(f32)

    g_packed = to_rows(d_packed)
    g_plain = g_packed[..., :plain_cols].reshape(ctx_count, piece, own_heads, DN)
    g_rope = g_packed[..., plain_cols : plain_cols + rope_cols]
    g_rope = g_rope.reshape(ctx_count, piece, own_heads, DR)
    g_query = jnp.concatenate([g_plain, g_rope], -1).transpose(1, 0, 2, 3).reshape(piece, -1)
    g_latent_in = g_packed[..., plain_cols + rope_cols :].transpose(1, 0, 2).reshape(piece, -1)
    g_latent_out = to_rows(d_latent_up)
    g_latent_out = g_latent_out.transpose(1, 0, 2).reshape(LAT // devices, -1)

    early = jnp.concatenate(
        [
            d_gain_ffn.reshape(devices, piece),
            d_router_proj.reshape(devices, piece * experts),
            jnp.broadcast_to(loss_part, (devices, 1)),
        ],
        1,
    )
    early = lax.psum_scatter(early, ("ctx", "shard"), scatter_dimension=0, tiled=True)[0]
    g_ffn = early[:piece]
    g_router = early[piece : piece + piece * experts].reshape(piece, experts)
    loss = early[-1] / (rows * devices * width)
    late = jnp.concatenate(
        [d_gain_attn.reshape(devices, piece), d_gain_latent.reshape(devices, -1)], 1
    )
    late = lax.psum_scatter(late, ("ctx", "shard"), scatter_dimension=0, tiled=True)[0]
    g_attn = late[:piece]
    g_latent = late[piece:]

    return (
        final.astype(bf16)[None],
        loss,
        token_grad[None],
        g_attn,
        g_query,
        g_latent_in,
        g_latent,
        g_latent_out,
        g_attn_out,
        g_ffn,
        g_router,
        g_gate,
        g_up,
        g_down,
        d_expert[0][None],
        d_expert[1][None],
        d_expert[2][None],
    )


def solution(mesh):
    in_specs = (
        P("shard", "ctx", None),
        P("shard", "ctx", None),
        P("shard", "ctx", None),
        P("shard"),
        P("shard", None),
        P("shard", None),
        P("shard"),
        P("shard", None),
        P("shard", None),
        P("shard"),
        P("shard", None),
        P("shard", None),
        P("shard", None),
        P("shard", None),
        P(("ctx", "shard"), None, None),
        P(("ctx", "shard"), None, None),
        P(("ctx", "shard"), None, None),
    )
    out_specs = (
        P("shard", "ctx", None),
        P(),
        P("shard", "ctx", None),
        P(("ctx", "shard")),
        P(("ctx", "shard"), None),
        P(("ctx", "shard"), None),
        P(("ctx", "shard")),
        P(("ctx", "shard"), None),
        P(("ctx", "shard"), None),
        P(("ctx", "shard")),
        P(("ctx", "shard"), None),
        P(("ctx", "shard"), None),
        P(("ctx", "shard"), None),
        P(("ctx", "shard"), None),
        P(("ctx", "shard"), None, None),
        P(("ctx", "shard"), None, None),
        P(("ctx", "shard"), None, None),
    )
    return jax.shard_map(
        on_device, mesh=mesh, in_specs=in_specs, out_specs=out_specs, check_vma=False
    )
```

```python
import functools

import jax
import jax.numpy as jnp
from jax import lax
from jax.experimental import pallas as pl
from jax.experimental.pallas import tpu as pltpu
from jax.sharding import PartitionSpec as P

H = 16
DN = 128
DR = 64
DV = 128
LAT = 512
TOP = 6
BLOCK = 256
LANES = 128

epsilon = 1e-06
base_freq = 10000.0
f32 = jnp.float32
bf16 = jnp.bfloat16


def tables(position, width):
    half = width // 2
    freqs = base_freq ** (-jnp.arange(half, dtype=f32) / half)
    angle = position.astype(f32)[:, None] * freqs[None, :]
    return (jnp.cos(angle), jnp.sin(angle))


def rotate(values, cosine, sine):
    half = values.shape[-1] // 2
    first = values[..., :half]
    second = values[..., half:]
    return jnp.concatenate([first * cosine - second * sine, second * cosine + first * sine], -1)


def rotate_back(grads, cosine, sine):
    return rotate(grads, cosine, -sine)


def inverse_root(values):
    return lax.rsqrt(jnp.mean(values * values, axis=-1, keepdims=True) + epsilon)


def norm_back(values, factor, gain, grads):
    scaled = grads * gain
    d_values = factor * scaled - values * factor**3 * jnp.mean(
        values * scaled, axis=-1, keepdims=True
    )
    return (d_values, jnp.sum(grads * values * factor, axis=0))


def silu_parts(values):
    sigma = jax.nn.sigmoid(values)
    return (values * sigma, sigma * (1.0 + values * (1.0 - sigma)))


def mm(left, right):
    return jnp.dot(left, right, preferred_element_type=f32)


def mm_nt(left, right):
    return lax.dot_general(left, right, (((1,), (1,)), ((), ())), preferred_element_type=f32)


def mm_tn(left, right):
    return lax.dot_general(left, right, (((0,), (0,)), ((), ())), preferred_element_type=f32)


def core_swap(value):
    count = lax.axis_size("ctx")
    return lax.ppermute(value, "ctx", [(i, i ^ 1) for i in range(count)])


def x_shift(value):
    count = lax.axis_size("ctx")
    return lax.ppermute(value, "ctx", [(i, (i + 2) % count) for i in range(count)])


def half_swap(value):
    count = lax.axis_size("shard")
    return lax.ppermute(value, "shard", [(i, i ^ 1) for i in range(count)])


def both_halves(value):
    count = lax.axis_size("shard")
    groups = [[i, i + 1] for i in range(0, count, 2)]
    return lax.all_gather(value, "shard", axis=0, tiled=False, axis_index_groups=groups)


def q_shift(value):
    count = lax.axis_size("shard")
    return lax.ppermute(value, "shard", [(i, (i + 2) % count) for i in range(count)])


def ring_sum(terms, shift, each=None):
    if len(terms) == 1:
        return terms[0].astype(f32)
    total = terms[1]
    for place, term in enumerate(list(terms[2:]) + [terms[0]]):
        total = shift(total.astype(bf16)).astype(f32) + term.astype(f32)
        if each is not None:
            total = each(place, total)
    return total


def gather_x(block):
    found = [block]
    for _ in range(lax.axis_size("ctx") // 2 - 1):
        found.append(x_shift(found[-1]))
    return [[item, core_swap(item)] for item in found]


def scatter_x(terms, last=None):
    pairs = [item[0].astype(f32) + core_swap(item[1].astype(bf16)).astype(f32) for item in terms]
    if last is not None:
        pairs[0] = last(pairs[0])
    return ring_sum(pairs, x_shift)


def place_of(dx, dc):
    ctx = lax.axis_index("ctx")
    chips = lax.axis_size("ctx") // 2
    return ((ctx // 2 - dx + chips) % chips) * 2 + (ctx % 2 + dc) % 2


def sum_ctx(value):
    total = value.astype(f32) + core_swap(value.astype(bf16)).astype(f32)
    moving = total.astype(bf16)
    for _ in range(lax.axis_size("ctx") // 2 - 1):
        moving = x_shift(moving)
        total = total + moving.astype(f32)
    return total


def scatter_ctx(full):
    count = lax.axis_size("ctx")
    rows = full.shape[0] // count
    terms = [
        [lax.dynamic_slice_in_dim(full, place_of(dx, dc) * rows, rows, 0) for dc in range(2)]
        for dx in range(count // 2)
    ]
    return scatter_x(terms)


def after(value, *others):
    operands = [value] + jax.tree.leaves(others)
    anywhere = pl.BlockSpec(memory_space=pl.ANY)
    return pl.pallas_call(
        lambda *refs: None,
        in_specs=[anywhere] * len(operands),
        out_specs=anywhere,
        out_shape=jax.ShapeDtypeStruct(value.shape, value.dtype),
        input_output_aliases={0: 0},
        name="after",
    )(*operands)


def both_of(own, other, bit):
    first = jnp.where(bit == 0, own, other)
    second = jnp.where(bit == 0, other, own)
    return jnp.concatenate([first, second], 0)


def ring_full(block, shift, count, me, each=None):
    if count == 1:
        return block
    rows = block.shape[0]
    full = jnp.zeros((count * rows,) + block.shape[1:], block.dtype)
    for step in range(count):
        if step:
            block = shift(block)
            if each is not None:
                block = each(block)
        full = lax.dynamic_update_slice_in_dim(full, block, ((me - step + count) % count) * rows, 0)
    return full


def gather_shard_from(pair, each=None):
    ring = lax.axis_size("shard") // 2
    return ring_full(pair, q_shift, ring, lax.axis_index("shard") // 2, each)


def gather_ctx_rows(block, between=None):
    ctx = lax.axis_index("ctx")
    chips = lax.axis_size("ctx") // 2
    lane = ring_full(block, x_shift, chips, ctx // 2)
    if between is not None:
        lane = between(lane)
    other = core_swap(lane)
    shape = (chips, 1) + block.shape
    lane, other = lane.reshape(shape), other.reshape(shape)
    first = jnp.where(ctx % 2 == 0, lane, other)
    second = jnp.where(ctx % 2 == 0, other, lane)
    return jnp.concatenate([first, second], 1).reshape((-1,) + block.shape[1:])


def all_sum(value):
    value = lax.all_to_all(value, ("ctx", "shard"), split_axis=0, concat_axis=0, tiled=True)
    return jnp.sum(value, axis=0)


def ring_shard(full, each=None):
    ring = lax.axis_size("shard") // 2
    me = lax.axis_index("shard") // 2
    full = full.reshape((ring, 2) + full.shape[1:])
    terms = [lax.dynamic_index_in_dim(full, (me - dq + ring) % ring, 0, False) for dq in range(ring)]
    return ring_sum(terms, q_shift, each)


def swap_halves(value):
    bit = lax.axis_index("shard") % 2
    own = lax.dynamic_index_in_dim(value, bit, 0, False)
    other = lax.dynamic_index_in_dim(value, 1 - bit, 0, False)
    return own.astype(f32) + half_swap(other.astype(bf16)).astype(f32)


def attn_parts(q_ref, r_ref, p_ref, k_ref, block, scale):
    size = (block + 1) * BLOCK
    at = pl.ds(block * BLOCK, BLOCK)
    query = q_ref[at, :]
    rope = r_ref[0, at, :]
    keys = p_ref[0:size, 0:DN]
    values = p_ref[0:size, DN : DN + DV]
    key_rope = k_ref[0:size, :]
    scores = (mm_nt(query, keys) + mm_nt(rope, key_rope)) * scale
    weights = jnp.exp(scores - jnp.max(scores, axis=-1, keepdims=True))
    probs = weights / jnp.sum(weights, axis=-1, keepdims=True)
    return query, rope, keys, values, key_rope, probs, size, at


def attn_fwd_kernel(scale, q_ref, r_ref, p_ref, k_ref, o_ref):
    for block in range(q_ref.shape[0] // BLOCK):
        _, _, _, values, _, probs, _, at = attn_parts(q_ref, r_ref, p_ref, k_ref, block, scale)
        o_ref[at, :] = mm(probs.astype(bf16), values).astype(bf16)


def attn_bwd_kernel(scale, q_ref, r_ref, p_ref, k_ref, g_ref, dq_ref, dr_ref, dp_ref, dk_ref, sum_ref):
    @pl.when(pl.program_id(0) == 0)
    def _():
        dk_ref[...] = jnp.zeros_like(dk_ref)

    sum_ref[...] = jnp.zeros_like(sum_ref)
    for block in range(q_ref.shape[0] // BLOCK):
        query, rope, keys, values, key_rope, probs, size, at = attn_parts(
            q_ref, r_ref, p_ref, k_ref, block, scale
        )
        grad = g_ref[at, :]
        low = probs.astype(bf16)
        d_probs = mm_nt(grad, values)
        d_scores = probs * (d_probs - jnp.sum(probs * d_probs, axis=-1, keepdims=True))
        d_scores = d_scores.astype(bf16)
        dq_ref[at, :] = (mm(d_scores, keys) * scale).astype(bf16)
        dr_ref[0, at, :] = mm(d_scores, key_rope) * scale
        sum_ref[0:size, 0:DN] += mm_tn(d_scores, query) * scale
        sum_ref[0:size, DN : DN + DV] += mm_tn(low, grad)
        dk_ref[0:size, :] += mm_tn(d_scores, rope) * scale
    dp_ref[...] = sum_ref[...].astype(bf16)


def attn_specs(seq):
    return [
        pl.BlockSpec((seq, DN), lambda i: (0, i)),
        pl.BlockSpec((1, seq, DR), lambda i: (i, 0, 0)),
        pl.BlockSpec((seq, DN + DV), lambda i: (0, i)),
        pl.BlockSpec((seq, DR), lambda i: (0, 0)),
    ]


def attend(query, rope, pairs, key_rope, scale):
    seq = query.shape[0]
    heads = rope.shape[0]
    return pl.pallas_call(
        functools.partial(attn_fwd_kernel, scale),
        grid=(heads,),
        in_specs=attn_specs(seq),
        out_specs=pl.BlockSpec((seq, DV), lambda i: (0, i)),
        out_shape=jax.ShapeDtypeStruct((seq, heads * DV), bf16),
        compiler_params=pltpu.CompilerParams(vmem_limit_bytes=40 * 1024 * 1024),
        name="attend",
    )(query, rope, pairs, key_rope)


def attend_back(query, rope, pairs, key_rope, grad, scale):
    seq = query.shape[0]
    heads = rope.shape[0]
    return pl.pallas_call(
        functools.partial(attn_bwd_kernel, scale),
        grid=(heads,),
        in_specs=attn_specs(seq) + [pl.BlockSpec((seq, DV), lambda i: (0, i))],
        out_specs=[
            pl.BlockSpec((seq, DN), lambda i: (0, i)),
            pl.BlockSpec((1, seq, DR), lambda i: (i, 0, 0)),
            pl.BlockSpec((seq, DN + DV), lambda i: (0, i)),
            pl.BlockSpec((seq, DR), lambda i: (0, 0)),
        ],
        out_shape=[
            jax.ShapeDtypeStruct((seq, heads * DN), bf16),
            jax.ShapeDtypeStruct((heads, seq, DR), f32),
            jax.ShapeDtypeStruct((seq, heads * (DN + DV)), bf16),
            jax.ShapeDtypeStruct((seq, DR), f32),
        ],
        scratch_shapes=[pltpu.VMEM((seq, DN + DV), f32)],
        compiler_params=pltpu.CompilerParams(vmem_limit_bytes=40 * 1024 * 1024),
        name="attend_back",
    )(query, rope, pairs, key_rope, grad)


def pick_of(info, tri, expert, experts, capacity):
    lanes = lax.broadcasted_iota(jnp.int32, (8, info.shape[1]), 1)
    mine = ((lanes == expert) | (lanes == experts + expert)).astype(f32).astype(bf16)
    weights = mm_nt(mine, info)[0:1, :]
    chosen = weights >= 0.0
    slot = mm(jnp.broadcast_to(chosen.astype(f32).astype(bf16), (8, info.shape[0])), tri)[0:1, :]
    place = lax.broadcasted_iota(jnp.int32, (capacity, info.shape[0]), 0).astype(f32) + 1.0
    pick = chosen & (slot == place)
    weight_row = jnp.sum(jnp.where(pick, weights, 0.0), axis=-1, keepdims=True)
    return pick.astype(f32).astype(bf16), weight_row


def triangle(rows):
    first = lax.broadcasted_iota(jnp.int32, (rows, rows), 0)
    second = lax.broadcasted_iota(jnp.int32, (rows, rows), 1)
    return (first <= second).astype(f32).astype(bf16)


def start_copies(sources, targets, sems, first):
    copies = [
        pltpu.make_async_copy(source, target, sems.at[first + i])
        for i, (source, target) in enumerate(zip(sources, targets))
    ]
    for item in copies:
        item.start()
    return copies


def wait_all(copies):
    for item in copies:
        item.wait()


def taker(refs):
    refs = list(refs)

    def take(count):
        found = refs[:count]
        del refs[:count]
        return found

    return take


WEIGHT_ORDER = (0, 2, 4, 1, 3, 5)


def halves_of(refs, other):
    return [ref for i in range(3) for ref in (refs[i], refs[3].at[other, i])]


def moe_fwd_kernel(dims, expert_ref, *refs):
    index, blocks, rows, width, experts, capacity, aliased = dims
    take = taker(refs)
    block_refs = take(blocks)
    weight_refs = halves_of(take(4), expert_ref[1])
    shared_refs = take(3)
    take(aliased)
    outs = take(blocks)
    keep_refs = take(6)
    flat, out, taken, gates, ups, scaled, shared_gates, shared_ups, made = take(9)
    weights = take(6)
    shared = take(3)
    (sems,) = take(1)
    picked = blocks * capacity
    here = pl.ds(index * picked, picked)
    tokens = pl.ds(index * blocks * rows, blocks * rows)
    spans = [pl.ds(b * rows, rows) for b in range(blocks)]
    arriving = start_copies(block_refs, [flat.at[span, :] for span in spans], sems, 0)
    moving = start_copies(
        [weight_refs[i] for i in WEIGHT_ORDER], [weights[i] for i in WEIGHT_ORDER], sems, blocks
    )
    moving = dict(zip(WEIGHT_ORDER, moving))
    rest = start_copies(shared_refs, shared, sems, blocks + 6)
    expert = expert_ref[0]
    tri = triangle(rows)
    picks = []
    weight_rows = []
    for b in range(blocks):
        arriving[b].wait()
        pick, weight_row = pick_of(flat[spans[b], width:], tri, expert, experts, capacity)
        picks.append(pick)
        weight_rows.append(weight_row)
        taken[pl.ds(b * capacity, capacity), :] = mm(pick, flat[spans[b], 0:width]).astype(bf16)
    leaving = start_copies([taken], [keep_refs[0].at[here, :]], sems, blocks + 9)
    weight_row = jnp.concatenate(weight_rows, 0)
    for side in range(2):
        moving[side].wait()
        gate = mm_nt(taken[...], weights[side][...])
        gates[side] = gate.astype(bf16)
        act = gate * jax.nn.sigmoid(gate) * weight_row
        moving[2 + side].wait()
        up = mm_nt(taken[...], weights[2 + side][...])
        ups[side] = up.astype(bf16)
        scaled[side] = (act * up).astype(bf16)
        moving[4 + side].wait()
        if side:
            made[...] += mm(scaled[side], weights[4 + side][...])
        else:
            made[...] = mm(scaled[side], weights[4 + side][...])
    leaving += start_copies(
        [gates, ups, scaled], [ref.at[:, here, :] for ref in keep_refs[1:4]], sems, blocks + 10
    )
    wait_all(rest)
    gate = mm_nt(flat[:, 0:width], shared[0][...])
    up = mm_nt(flat[:, 0:width], shared[1][...])
    shared_gates[...] = gate
    shared_ups[...] = up
    leaving += start_copies(
        [shared_gates, shared_ups], [ref.at[tokens, :] for ref in keep_refs[4:6]], sems, blocks + 13
    )
    hidden = (gate * jax.nn.sigmoid(gate) * up).astype(bf16)
    for b in range(blocks):
        rows_of = made[pl.ds(b * capacity, capacity), :].astype(bf16)
        out[spans[b], :] = (
            mm_tn(picks[b], rows_of) + mm(hidden[b * rows : (b + 1) * rows, :], shared[2][...])
        ).astype(bf16)
        leaving += start_copies([out.at[spans[b], :]], [outs[b]], sems, blocks + 15 + b)
    wait_all(leaving)


def moe_bwd_kernel(dims, expert_ref, *refs):
    index, blocks, rows, width, experts, capacity, aliased = dims
    take = taker(refs)
    error_refs = take(blocks)
    block_refs = take(blocks)
    weight_refs = halves_of(take(4), expert_ref[1])
    shared_refs = take(3)
    kept_refs = take(4)
    take(aliased)
    outs = take(blocks)
    sum_refs = take(3)
    keep_refs = take(3)
    errors, flat, taken, gates, ups, d_gates, d_ups, shared_gates, shared_ups, made = take(10)
    sums = take(3)
    weights = take(6)
    shared = take(3)
    (sems,) = take(1)
    picked = blocks * capacity
    here = pl.ds(index * picked, picked)
    tokens = pl.ds(index * blocks * rows, blocks * rows)
    spans = [pl.ds(b * rows, rows) for b in range(blocks)]
    arriving = start_copies(error_refs, [errors.at[span, 0:width] for span in spans], sems, 0)
    inputs = start_copies(block_refs, [flat.at[span, :] for span in spans], sems, blocks)
    first = 2 * blocks
    order = (4, 0, 2, 5, 1, 3)
    kept = start_copies(
        [ref.at[:, here, :] for ref in kept_refs[0:2]], [gates, ups], sems, first
    )
    moving = start_copies(
        [weight_refs[i] for i in order], [weights[i] for i in order], sems, first + 2
    )
    moving = dict(zip(order, moving))
    kept_shared = start_copies(
        [ref.at[tokens, :] for ref in kept_refs[2:4]], [shared_gates, shared_ups], sems, first + 8
    )
    rest = start_copies(shared_refs, shared, sems, first + 10)
    first = first + 13
    expert = expert_ref[0]
    tri = triangle(rows)
    picks = []
    weight_rows = []
    for b in range(blocks):
        inputs[b].wait()
        arriving[b].wait()
        pick, weight_row = pick_of(flat[spans[b], width:], tri, expert, experts, capacity)
        picks.append(pick)
        weight_rows.append(weight_row)
        taken[pl.ds(b * capacity, capacity), :] = mm(pick, errors[spans[b], 0:width]).astype(bf16)
    leaving = start_copies([taken], [keep_refs[0].at[here, :]], sems, first)
    weight_row = jnp.concatenate(weight_rows, 0)
    wait_all(kept)
    d_weight = 0.0
    for side in range(2):
        moving[4 + side].wait()
        d_plain = mm_nt(taken[...], weights[4 + side][...])
        gate = gates[side].astype(f32)
        up = ups[side].astype(f32)
        act, slope = silu_parts(gate)
        d_weight = d_weight + jnp.sum(act * up * d_plain, axis=-1, keepdims=True)
        d_hidden = d_plain * weight_row
        d_gates[side] = (d_hidden * up * slope).astype(bf16)
        d_ups[side] = (d_hidden * act).astype(bf16)
        moving[side].wait()
        moving[2 + side].wait()
        back = mm(d_gates[side], weights[side][...]) + mm(d_ups[side], weights[2 + side][...])
        if side:
            made[...] += back
        else:
            made[...] = back
    leaving += start_copies(
        [d_gates, d_ups], [ref.at[:, here, :] for ref in keep_refs[1:3]], sems, first + 1
    )
    wait_all(rest)
    wait_all(kept_shared)
    act, slope = silu_parts(shared_gates[...])
    shared_up = shared_ups[...]
    d_hidden = mm_nt(errors[:, 0:width], shared[2][...])
    d_gate = (d_hidden * shared_up * slope).astype(bf16)
    d_up = (d_hidden * act).astype(bf16)
    sums[0][...] = mm_tn(d_gate, flat[:, 0:width])
    sums[1][...] = mm_tn(d_up, flat[:, 0:width])
    sums[2][...] = mm_tn((act * shared_up).astype(bf16), errors[:, 0:width])
    leaving += start_copies(sums, sum_refs, sems, first + 3)
    info_cols = flat.shape[1] - width
    lanes = lax.broadcasted_iota(jnp.int32, (capacity, info_cols), 1)
    for b in range(blocks):
        rows_of = made[pl.ds(b * capacity, capacity), :].astype(bf16)
        span = slice(b * rows, (b + 1) * rows)
        errors[spans[b], 0:width] = (
            mm_tn(picks[b], rows_of)
            + mm(d_gate[span, :], shared[0][...])
            + mm(d_up[span, :], shared[1][...])
        ).astype(bf16)
        column = d_weight[b * capacity : (b + 1) * capacity, :]
        high = column.astype(bf16).astype(f32)
        found = jnp.where(lanes == expert, high, 0.0)
        found = jnp.where(lanes == experts + expert, column - high, found)
        errors[spans[b], width:] = mm_tn(picks[b], found.astype(bf16)).astype(bf16)
        leaving += start_copies([errors.at[spans[b], :]], [outs[b]], sems, first + 6 + b)
    wait_all(leaving)


def moe_call(kernel, dims, expert, groups, before, out_blocks, out_plain, out_kept, scratch, copies, cost, name):
    operands = [item for group in groups for item in group] + list(before)
    anywhere = pl.BlockSpec(memory_space=pl.ANY)
    shapes = out_blocks + out_plain + out_kept
    first = 1 + len(operands) - len(before)
    return pl.pallas_call(
        functools.partial(kernel, dims + (len(before),)),
        in_specs=[pl.BlockSpec(memory_space=pltpu.SMEM)] + [anywhere] * len(operands),
        out_specs=[anywhere] * len(shapes),
        out_shape=shapes,
        scratch_shapes=scratch + [pltpu.SemaphoreType.DMA((copies,))],
        input_output_aliases={
            first + i: len(out_blocks) + len(out_plain) + i for i in range(len(before))
        },
        compiler_params=pltpu.CompilerParams(vmem_limit_bytes=60 * 1024 * 1024),
        cost_estimate=cost,
        name=name,
    )(expert, *operands)


def moe_fwd(index, chunks, expert, experts, capacity, blocks, weights, shared, kept):
    count = len(blocks)
    rows = blocks[0].shape[0]
    half, width = weights[0].shape
    hidden = shared[0].shape[0]
    taken = count * capacity
    tokens = count * rows
    shape = jax.ShapeDtypeStruct
    result = moe_call(
        moe_fwd_kernel,
        (index, count, rows, width, experts, capacity),
        expert,
        (blocks, weights, shared),
        [] if kept is None else kept,
        [shape((rows, width), bf16)] * count,
        [],
        [shape((chunks * taken, width), bf16)]
        + [shape((2, chunks * taken, half), bf16)] * 3
        + [shape((chunks * tokens, hidden), f32)] * 2,
        [
            pltpu.VMEM((tokens, blocks[0].shape[1]), bf16),
            pltpu.VMEM((tokens, width), bf16),
            pltpu.VMEM((taken, width), bf16),
            pltpu.VMEM((2, taken, half), bf16),
            pltpu.VMEM((2, taken, half), bf16),
            pltpu.VMEM((2, taken, half), bf16),
            pltpu.VMEM((tokens, hidden), f32),
            pltpu.VMEM((tokens, hidden), f32),
            pltpu.VMEM((taken, width), f32),
        ]
        + [pltpu.VMEM((half, width), bf16)] * 6
        + [pltpu.VMEM((hidden, width), bf16)] * 3,
        2 * count + 15,
        pl.CostEstimate(flops=0, bytes_accessed=0, transcendentals=0),
        "moe_fwd",
    )
    return list(result[:count]), list(result[count:])


def moe_bwd(index, chunks, expert, experts, capacity, errors, blocks, weights, shared, kept, before):
    count = len(blocks)
    rows = blocks[0].shape[0]
    half, width = weights[0].shape
    hidden = shared[0].shape[0]
    taken = count * capacity
    tokens = count * rows
    shape = jax.ShapeDtypeStruct
    result = moe_call(
        moe_bwd_kernel,
        (index, count, rows, width, experts, capacity),
        expert,
        (errors, blocks, weights, shared, kept),
        [] if before is None else before,
        [shape(blocks[0].shape, bf16)] * count,
        [shape((hidden, width), f32)] * 3,
        [shape((chunks * taken, width), bf16)] + [shape((2, chunks * taken, half), bf16)] * 2,
        [
            pltpu.VMEM((tokens, blocks[0].shape[1]), bf16),
            pltpu.VMEM((tokens, blocks[0].shape[1]), bf16),
            pltpu.VMEM((taken, width), bf16),
            pltpu.VMEM((2, taken, half), bf16),
            pltpu.VMEM((2, taken, half), bf16),
            pltpu.VMEM((2, taken, half), bf16),
            pltpu.VMEM((2, taken, half), bf16),
            pltpu.VMEM((tokens, hidden), f32),
            pltpu.VMEM((tokens, hidden), f32),
            pltpu.VMEM((taken, width), f32),
        ]
        + [pltpu.VMEM((hidden, width), f32)] * 3
        + [pltpu.VMEM((half, width), bf16)] * 6
        + [pltpu.VMEM((hidden, width), bf16)] * 3,
        3 * count + 19,
        pl.CostEstimate(flops=0, bytes_accessed=0, transcendentals=0),
        "moe_bwd",
    )
    return list(result[:count]), list(result[count : count + 3]), list(result[count + 3 :])


def on_device(
    tokens,
    target,
    routes,
    attn_gain,
    w_query,
    w_latent_in,
    latent_gain,
    w_latent_out,
    w_attn_out,
    ffn_gain,
    w_router,
    shared_gate,
    shared_up,
    shared_down,
    expert_gate,
    expert_up,
    expert_down,
):
    rows = tokens.shape[1]
    width = tokens.shape[2]
    ctx_count = lax.axis_size("ctx")
    shard_count = lax.axis_size("shard")
    chips = ctx_count // 2
    ring = shard_count // 2
    experts = ctx_count * ring
    capacity = max(2, (rows * TOP * 4 + experts * 3 - 1) // (experts * 3))
    seq_len = rows * ctx_count
    own_heads = H // ctx_count
    scale = (DN + DR) ** (-0.5)
    ctx = lax.axis_index("ctx")
    shard = lax.axis_index("shard")
    expert = ctx * ring + shard // 2
    devices = ctx_count * shard_count
    piece = width // devices

    depth = w_query.shape[0]
    lat_rows = latent_gain.shape[0]
    part = depth // ctx_count
    lat_part = lat_rows // ctx_count
    half_bit = shard % 2
    small = jnp.concatenate(
        [
            w_latent_in,
            attn_gain[:, None],
            ffn_gain[:, None],
            jnp.pad(latent_gain.reshape(ctx_count, lat_part), ((0, 0), (0, part - lat_part)))
            .reshape(depth, 1),
            w_router,
        ],
        1,
    )
    small = jnp.pad(small, ((0, 0), (0, -small.shape[1] % LANES)))
    small = lax.dynamic_slice_in_dim(small, ctx * part, part, 0)
    own_query = lax.dynamic_slice_in_dim(
        w_query, ctx * own_heads * (DN + DR), own_heads * (DN + DR), 1
    ).reshape(depth, own_heads, DN + DR)
    plain_cols = own_heads * DN
    rope_cols = own_heads * DR
    packed = jnp.concatenate(
        [
            own_query[..., :DN].reshape(depth, plain_cols),
            own_query[..., DN:].reshape(depth, rope_cols),
        ],
        1,
    )
    own_pairs = own_heads * (DN + DV)
    up_piece = lax.dynamic_slice_in_dim(w_latent_out, ctx * own_pairs, own_pairs, 1)
    packed = jnp.concatenate([packed, up_piece.reshape(depth, -1)], 1)
    packed_pair = both_of(packed, half_swap(packed), half_bit)
    out_piece = 0.0
    for j in range(ctx_count):
        moves = []
        for t in range(shard_count):
            to = t * ctx_count + j
            base = (to // shard_count) * shard_count
            moves.append((base + t, to))
        out_piece = out_piece + lax.ppermute(
            w_attn_out[j * piece : (j + 1) * piece], ("ctx", "shard"), moves
        )
    out_pair = both_of(out_piece, half_swap(out_piece), half_bit)

    slice_rows = shared_down.shape[0] // ctx_count
    down_own = lax.dynamic_slice_in_dim(shared_down, ctx * slice_rows, slice_rows, 0)
    both = jnp.stack([shared_gate, shared_up], 0).reshape(
        2, depth, shard_count, ctx_count, slice_rows
    )
    both = lax.dynamic_index_in_dim(both, ctx, 3, False)
    both = both.transpose(2, 0, 3, 1).reshape(shard_count, 2 * slice_rows, depth)
    both = lax.all_to_all(both, "shard", split_axis=0, concat_axis=0, tiled=True)
    both = both.transpose(1, 0, 2).reshape(2 * slice_rows, width)
    slices = jnp.concatenate([both, down_own], 0)
    slices = jnp.stack([slices, half_swap(slices)], 0).reshape(2, 3, slice_rows, width)
    shared_all = [slices[:, i].reshape(2 * slice_rows, width) for i in range(3)]

    small = gather_shard_from(both_of(small, half_swap(small), half_bit))
    small = after(small, both)
    small = gather_ctx_rows(small).reshape(ctx_count, shard_count, part, -1)
    latent_cols = LAT + DR
    small_gains = small[..., latent_cols : latent_cols + 3].transpose(3, 1, 0, 2)
    gain_attn = small_gains[0].reshape(width).astype(f32)
    gain_ffn = small_gains[1].reshape(width).astype(f32)
    gain_latent = small_gains[2, :, :, :lat_part].reshape(LAT).astype(f32)
    small = small.transpose(1, 0, 2, 3).reshape(width, -1)
    latent_down = small[:, :latent_cols]
    router_proj = small[:, latent_cols + 3 : latent_cols + 3 + experts]

    own_half = [expert_gate[0].T, expert_up[0].T, expert_down[0]]
    weights_all = own_half + [both_halves(jnp.stack(own_half, 0))]

    gathered = gather_shard_from(packed_pair)
    plain_proj = gathered[:, :plain_cols]
    rope_proj = gathered[:, plain_cols : plain_cols + rope_cols]
    packed = gathered[:, : plain_cols + rope_cols]
    latent_up = gathered[:, plain_cols + rope_cols :].reshape(LAT, own_pairs)
    out_proj = gather_shard_from(after(out_pair, gathered, slices))

    source = tokens[0].astype(f32)
    factor_attn = inverse_root(source)
    all_source = gather_ctx_rows(tokens[0]).astype(f32)
    attn_in = (all_source * inverse_root(all_source) * gain_attn).astype(bf16)
    cosine, sine = tables(jnp.arange(seq_len), DR)
    query = mm(attn_in, plain_proj).astype(bf16)
    query_rope = jnp.einsum(
        "td,dhk->htk",
        attn_in,
        rope_proj.reshape(width, own_heads, DR),
        preferred_element_type=f32,
    )
    query_rope = rotate(query_rope, cosine, sine).astype(bf16)
    latent_raw = mm(attn_in, latent_down)
    latent_part = latent_raw[:, :LAT]
    latent = (latent_part * inverse_root(latent_part) * gain_latent).astype(bf16)
    key_rope = rotate(latent_raw[:, LAT:], cosine, sine).astype(bf16)
    pairs = mm(latent, latent_up).astype(bf16)
    heads = attend(query, query_rope, pairs, key_rope, scale)
    middle = source + scatter_ctx(mm(heads, out_proj).astype(bf16))

    factor_ffn = inverse_root(middle)
    ffn_in = (middle * factor_ffn * gain_ffn).astype(bf16)
    router = jax.nn.softmax(mm(ffn_in, router_proj), axis=-1)
    chosen_any = jnp.any(
        routes[0][:, :, None] == jnp.arange(experts, dtype=jnp.int32)[None, None, :], axis=1
    )
    weight = jnp.where(chosen_any, router, -1.0)
    weight_high = weight.astype(bf16)
    weight_low = (weight - weight_high.astype(f32)).astype(bf16)
    info = jnp.concatenate(
        [
            weight_high,
            weight_low,
            jnp.zeros((rows, max(0, LANES - 2 * experts)), bf16),
        ],
        1,
    )
    info_cols = info.shape[1]

    expert_at = jnp.stack([expert, 1 - half_bit]).astype(jnp.int32)

    def through(block, work, last=None, each=None):
        gate = expert_at
        sums = []
        done = []
        for step in range(ring):
            if step:
                block = q_shift(block)
            if step > 1:
                block = after(block, done[-2])
            found = work(step, [item for pair in gather_x(block) for item in pair], gate)
            done.append(found[0])
            pairs = [
                found[2 * i].astype(f32) + core_swap(found[2 * i + 1]).astype(f32)
                for i in range(chips)
            ]
            waits = [pairs[-1]] + (sums[-1:] if step > 1 else [])
            if step == ring - 1 and last is not None:
                pairs[0] = last(pairs[0])
            sums.append(ring_sum(pairs, x_shift))
            gate = after(expert_at, waits)
        return ring_sum(sums, q_shift, each)

    in_chunks = []
    kept = None

    def forward(index, chunk, gate):
        nonlocal kept
        in_chunks.append(chunk)
        out, kept = moe_fwd(
            index, ring, gate, experts, capacity, chunk, weights_all, shared_all, kept
        )
        return out

    final = middle + through(jnp.concatenate([ffn_in, info], 1), forward)
    error = final - target[0].astype(f32)
    loss_part = jnp.sum(error * error)

    d_shared = []
    d_kept = None

    def backward(index, chunk, gate):
        nonlocal d_kept
        out, part, d_kept = moe_bwd(
            index,
            ring,
            gate,
            experts,
            capacity,
            chunk,
            in_chunks[index],
            weights_all,
            shared_all,
            [kept[1], kept[2], kept[4], kept[5]],
            d_kept,
        )
        d_shared.append(part)
        return out

    def half_grads(half):
        taken, scaled = kept[0], kept[3]
        d_taken, d_gates, d_ups = d_kept
        return (mm_tn(d_gates[half], taken), mm_tn(d_ups[half], taken), mm_tn(scaled[half], d_taken))

    block = error.astype(bf16)
    terms = []
    for step in range(ring):
        if step:
            block = q_shift(block)
        found = backward(step, [item for pair in gather_x(block) for item in pair], expert_at)
        pairs_of = [[found[2 * i], found[2 * i + 1]] for i in range(chips)]
        terms.append(scatter_x(pairs_of))
    d_all = ring_sum(terms, q_shift)
    for_other = [item.astype(bf16) for item in half_grads(1)]
    from_other = [both_halves(for_other[0]), both_halves(jnp.stack(for_other[1:], 0))]
    d_ffn = d_all[:, :width]
    d_info = d_all[:, width:]
    d_router = d_info[:, :experts] + d_info[:, experts : 2 * experts]
    d_router = jnp.where(chosen_any, d_router, 0.0)

    d_slices = jnp.stack([sum(item[i] for item in d_shared) for i in range(3)], 0)
    d_logits = (router * (d_router - jnp.sum(router * d_router, axis=-1, keepdims=True))).astype(
        bf16
    )
    d_router_proj = mm_tn(ffn_in, d_logits)
    d_ffn = d_ffn + mm_nt(d_logits, router_proj)
    d_middle_norm, d_gain_ffn = norm_back(middle, factor_ffn, gain_ffn, d_ffn)
    d_middle = error + d_middle_norm

    d_branch = gather_ctx_rows(d_middle.astype(bf16))
    d_out_proj = mm_tn(heads, d_branch).astype(bf16)
    d_heads = mm_nt(d_branch, out_proj).astype(bf16)
    d_heads = after(d_heads, d_out_proj, from_other[0])
    d_query, d_rope, d_pairs, d_key_rope = attend_back(
        query, query_rope, pairs, key_rope, d_heads, scale
    )
    d_latent_sum = jnp.concatenate([mm_nt(d_pairs, latent_up), d_key_rope], 1).astype(bf16)
    d_latent = sum_ctx(d_latent_sum)
    d_rope = rotate_back(d_rope, cosine, sine).astype(bf16)
    d_rope = d_rope.transpose(1, 0, 2).reshape(seq_len, rope_cols)
    d_query = after(jnp.concatenate([d_query, d_rope], 1), d_latent_sum)
    d_latent_part, _ = norm_back(
        latent_part, inverse_root(latent_part), gain_latent, d_latent[:, :LAT]
    )
    d_latent_raw = jnp.concatenate(
        [d_latent_part, rotate_back(d_latent[:, LAT:], cosine, sine)], -1
    ).astype(bf16)
    first = ctx * rows
    own_latent = lax.dynamic_slice_in_dim(latent_part, first, rows, 0)
    own_grads = lax.dynamic_slice_in_dim(d_latent, first, rows, 0)[:, :LAT]
    d_gain_latent = jnp.sum(own_grads * own_latent * inverse_root(own_latent), axis=0)
    latent_cols = (LAT + DR) // ctx_count
    d_latent_all = lax.dynamic_slice_in_dim(
        d_latent_raw, ctx * latent_cols, latent_cols, 1
    )
    d_packed = mm_tn(attn_in, d_query).astype(bf16)
    d_attn_in = scatter_ctx(
        mm_nt(after(d_query, d_packed), packed).astype(bf16)
    ) + mm_nt(lax.dynamic_slice_in_dim(d_latent_raw, first, rows, 0), latent_down)
    d_latent_up = mm_tn(latent, d_pairs)
    d_source_norm, d_gain_attn = norm_back(source, factor_attn, gain_attn, d_attn_in)
    token_grad = d_middle + d_source_norm

    def by_rows(value):
        cols = value.shape[1]
        return value.astype(bf16).reshape(ctx_count, shard_count, -1, cols).transpose(1, 0, 2, 3)

    d_latent_in = by_rows(mm_tn(attn_in, d_latent_all))
    d_latent_out = by_rows(d_latent_up)
    latent_shape = d_latent_in.shape
    d_latents = jnp.concatenate(
        [d_latent_in.reshape(latent_shape[:2] + (-1,)), d_latent_out.reshape(latent_shape[:2] + (-1,))],
        2,
    ).reshape(shard_count, ctx_count, -1, LANES)

    early = jnp.concatenate(
        [
            d_out_proj.reshape(shard_count, -1, LANES),
            by_rows(d_packed).reshape(shard_count, -1, LANES),
        ],
        1,
    )
    sum_early = ring_shard(early)
    sum_latents = ring_shard(d_latents)
    sums = [sum_early, sum_latents]
    flat = jnp.concatenate([item.astype(bf16).reshape(2, -1, LANES) for item in sums], 1)
    flat = swap_halves(flat)
    out_rows = d_out_proj.size // (shard_count * LANES)
    g_attn_out = flat[:out_rows].reshape(piece, width)
    flat = flat[out_rows:].astype(bf16)
    packed_rows = d_packed.size // (shard_count * LANES)
    flat = jnp.concatenate(
        [
            flat[:packed_rows].reshape(ctx_count, -1, LANES),
            flat[packed_rows:].reshape(ctx_count, -1, LANES),
        ],
        1,
    )
    flat = lax.all_to_all(flat, "ctx", split_axis=0, concat_axis=0, tiled=True).astype(f32)
    packed_rows = packed_rows // ctx_count
    g_packed = flat[:, :packed_rows].reshape(ctx_count, piece, -1)
    g_plain = g_packed[..., :plain_cols].reshape(ctx_count, piece, own_heads, DN)
    g_rope = g_packed[..., plain_cols:].reshape(ctx_count, piece, own_heads, DR)
    g_query = jnp.concatenate([g_plain, g_rope], -1).transpose(1, 0, 2, 3).reshape(piece, -1)
    g_latents = flat[:, packed_rows:].reshape(ctx_count, -1)
    g_latent_in = g_latents[:, : piece * latent_cols].reshape(ctx_count, piece, latent_cols)
    g_latent_in = g_latent_in.transpose(1, 0, 2).reshape(piece, -1)
    g_latent_out = g_latents[:, piece * latent_cols :].reshape(ctx_count, LAT // devices, -1)
    g_latent_out = g_latent_out.transpose(1, 0, 2).reshape(LAT // devices, -1)

    from_other = [
        lax.dynamic_index_in_dim(after(item, late), 1 - half_bit, 0, False)
        for item, late in zip(from_other, (d_packed, d_latents))
    ]
    from_other = [from_other[0], from_other[1][0], from_other[1][1]]
    d_expert = [item + other.astype(f32) for item, other in zip(half_grads(0), from_other)]
    d_expert = [d_expert[0].T, d_expert[1].T, d_expert[2]]

    moves = []
    for a in range(ctx_count):
        for b in range(shard_count):
            moves.append((a * shard_count + b, b * ctx_count + a))
    d_slices = after(d_slices, d_heads).reshape(3, 2, slice_rows, width)
    d_slices = d_slices[:, 0] + half_swap(d_slices[:, 1].astype(bf16)).astype(f32)
    d_slices = after(d_slices.astype(bf16), d_packed)
    g_down = lax.ppermute(d_slices[2], ("ctx", "shard"), moves)
    d_both = d_slices[:2].reshape(2, slice_rows, devices, piece)
    d_both = lax.all_to_all(
        d_both.transpose(2, 0, 1, 3).reshape(devices, 2 * slice_rows, piece),
        ("ctx", "shard"),
        split_axis=0,
        concat_axis=0,
        tiled=True,
    )
    g_down = after(g_down, d_latents).astype(f32)
    d_both = after(d_both, d_latents)
    d_both = d_both.reshape(ctx_count, shard_count, 2, slice_rows, piece)
    d_both = d_both.transpose(2, 4, 1, 0, 3).reshape(2, piece, -1).astype(f32)
    g_gate = d_both[0]
    g_up = d_both[1]

    small_sums = jnp.concatenate(
        [
            d_gain_ffn.reshape(devices, piece),
            d_router_proj.reshape(devices, piece * experts),
            d_gain_attn.reshape(devices, piece),
            d_gain_latent.reshape(devices, -1),
            jnp.broadcast_to(loss_part, (devices, 1)),
        ],
        1,
    )
    small_sums = all_sum(small_sums)
    g_ffn = small_sums[:piece]
    at = piece + piece * experts
    g_router = small_sums[piece:at].reshape(piece, experts)
    g_attn = small_sums[at : at + piece]
    g_latent = small_sums[at + piece : -1]
    loss = small_sums[-1] / (rows * devices * width)

    return (
        final.astype(bf16)[None],
        loss,
        token_grad[None],
        g_attn,
        g_query,
        g_latent_in,
        g_latent,
        g_latent_out,
        g_attn_out,
        g_ffn,
        g_router,
        g_gate,
        g_up,
        g_down,
        d_expert[0][None],
        d_expert[1][None],
        d_expert[2][None],
    )


def solution(mesh):
    in_specs = (
        P("shard", "ctx", None),
        P("shard", "ctx", None),
        P("shard", "ctx", None),
        P("shard"),
        P("shard", None),
        P("shard", None),
        P("shard"),
        P("shard", None),
        P("shard", None),
        P("shard"),
        P("shard", None),
        P("shard", None),
        P("shard", None),
        P("shard", None),
        P(("ctx", "shard"), None, None),
        P(("ctx", "shard"), None, None),
        P(("ctx", "shard"), None, None),
    )
    out_specs = (
        P("shard", "ctx", None),
        P(),
        P("shard", "ctx", None),
        P(("ctx", "shard")),
        P(("ctx", "shard"), None),
        P(("ctx", "shard"), None),
        P(("ctx", "shard")),
        P(("ctx", "shard"), None),
        P(("ctx", "shard"), None),
        P(("ctx", "shard")),
        P(("ctx", "shard"), None),
        P(("ctx", "shard"), None),
        P(("ctx", "shard"), None),
        P(("ctx", "shard"), None),
        P(("ctx", "shard"), None, None),
        P(("ctx", "shard"), None, None),
        P(("ctx", "shard"), None, None),
    )
    return jax.shard_map(
        on_device, mesh=mesh, in_specs=in_specs, out_specs=out_specs, check_vma=False
    )
```

```python
import functools

import jax
import jax.numpy as jnp
from jax import lax
from jax.experimental import pallas as pl
from jax.experimental.pallas import tpu as pltpu
from jax.sharding import PartitionSpec as P

H = 16
DN = 128
DR = 64
DV = 128
LAT = 512
TOP = 6
BLOCK = 256
LANES = 128

epsilon = 1e-06
base_freq = 10000.0
f32 = jnp.float32
bf16 = jnp.bfloat16


def tables(position, width):
    half = width // 2
    freqs = base_freq ** (-jnp.arange(half, dtype=f32) / half)
    angle = position.astype(f32)[:, None] * freqs[None, :]
    return (jnp.cos(angle), jnp.sin(angle))


def rotate(values, cosine, sine):
    half = values.shape[-1] // 2
    first = values[..., :half]
    second = values[..., half:]
    return jnp.concatenate([first * cosine - second * sine, second * cosine + first * sine], -1)


def rotate_back(grads, cosine, sine):
    return rotate(grads, cosine, -sine)


def inverse_root(values):
    return lax.rsqrt(jnp.mean(values * values, axis=-1, keepdims=True) + epsilon)


def norm_back(values, factor, gain, grads):
    scaled = grads * gain
    d_values = factor * scaled - values * factor**3 * jnp.mean(
        values * scaled, axis=-1, keepdims=True
    )
    return (d_values, jnp.sum(grads * values * factor, axis=0))


def silu_parts(values):
    sigma = jax.nn.sigmoid(values)
    return (values * sigma, sigma * (1.0 + values * (1.0 - sigma)))


def mm(left, right):
    return jnp.dot(left, right, preferred_element_type=f32)


def mm_nt(left, right):
    return lax.dot_general(left, right, (((1,), (1,)), ((), ())), preferred_element_type=f32)


def mm_tn(left, right):
    return lax.dot_general(left, right, (((0,), (0,)), ((), ())), preferred_element_type=f32)


def core_swap(value):
    count = lax.axis_size("ctx")
    return lax.ppermute(value, "ctx", [(i, i ^ 1) for i in range(count)])


def x_shift(value):
    count = lax.axis_size("ctx")
    return lax.ppermute(value, "ctx", [(i, (i + 2) % count) for i in range(count)])


def half_swap(value):
    count = lax.axis_size("shard")
    return lax.ppermute(value, "shard", [(i, i ^ 1) for i in range(count)])


def both_halves(value):
    count = lax.axis_size("shard")
    groups = [[i, i + 1] for i in range(0, count, 2)]
    return lax.all_gather(value, "shard", axis=0, tiled=False, axis_index_groups=groups)


def q_shift(value):
    count = lax.axis_size("shard")
    return lax.ppermute(value, "shard", [(i, (i + 2) % count) for i in range(count)])


def ring_sum(terms, shift, each=None):
    if len(terms) == 1:
        return terms[0].astype(f32)
    total = terms[1]
    for place, term in enumerate(list(terms[2:]) + [terms[0]]):
        total = shift(total.astype(bf16)).astype(f32) + term.astype(f32)
        if each is not None:
            total = each(place, total)
    return total


def gather_x(block):
    found = [block]
    for _ in range(lax.axis_size("ctx") // 2 - 1):
        found.append(x_shift(found[-1]))
    return [[item, core_swap(item)] for item in found]


def scatter_x(terms, last=None):
    pairs = [item[0].astype(f32) + core_swap(item[1].astype(bf16)).astype(f32) for item in terms]
    if last is not None:
        pairs[0] = last(pairs[0])
    return ring_sum(pairs, x_shift)


def place_of(dx, dc):
    ctx = lax.axis_index("ctx")
    chips = lax.axis_size("ctx") // 2
    return ((ctx // 2 - dx + chips) % chips) * 2 + (ctx % 2 + dc) % 2


def sum_cores(value):
    return (value.astype(f32) + core_swap(value.astype(bf16)).astype(f32)).astype(bf16)


def sum_chips(moving):
    total = moving.astype(f32)
    for _ in range(lax.axis_size("ctx") // 2 - 1):
        moving = x_shift(moving)
        total = total + moving.astype(f32)
    return total


def scatter_ctx(full):
    count = lax.axis_size("ctx")
    rows = full.shape[0] // count
    terms = [
        [lax.dynamic_slice_in_dim(full, place_of(dx, dc) * rows, rows, 0) for dc in range(2)]
        for dx in range(count // 2)
    ]
    return scatter_x(terms)


def after(value, *others):
    operands = [value] + jax.tree.leaves(others)
    anywhere = pl.BlockSpec(memory_space=pl.ANY)
    return pl.pallas_call(
        lambda *refs: None,
        in_specs=[anywhere] * len(operands),
        out_specs=anywhere,
        out_shape=jax.ShapeDtypeStruct(value.shape, value.dtype),
        input_output_aliases={0: 0},
        name="after",
    )(*operands)


def both_of(own, other, bit):
    first = jnp.where(bit == 0, own, other)
    second = jnp.where(bit == 0, other, own)
    return jnp.concatenate([first, second], 0)


def ring_full(block, shift, count, me, each=None):
    if count == 1:
        return block
    rows = block.shape[0]
    full = jnp.zeros((count * rows,) + block.shape[1:], block.dtype)
    for step in range(count):
        if step:
            block = shift(block)
            if each is not None:
                block = each(block)
        full = lax.dynamic_update_slice_in_dim(full, block, ((me - step + count) % count) * rows, 0)
    return full


def gather_shard_from(pair, each=None):
    ring = lax.axis_size("shard") // 2
    return ring_full(pair, q_shift, ring, lax.axis_index("shard") // 2, each)


def gather_ctx_rows(block, between=None):
    ctx = lax.axis_index("ctx")
    chips = lax.axis_size("ctx") // 2
    lane = ring_full(block, x_shift, chips, ctx // 2)
    if between is not None:
        lane = between(lane)
    other = core_swap(lane)
    shape = (chips, 1) + block.shape
    lane, other = lane.reshape(shape), other.reshape(shape)
    first = jnp.where(ctx % 2 == 0, lane, other)
    second = jnp.where(ctx % 2 == 0, other, lane)
    return jnp.concatenate([first, second], 1).reshape((-1,) + block.shape[1:])


def all_sum(value):
    value = lax.all_to_all(value, ("ctx", "shard"), split_axis=0, concat_axis=0, tiled=True)
    return jnp.sum(value, axis=0)


def ring_shard(full, each):
    ring = lax.axis_size("shard") // 2
    me = lax.axis_index("shard") // 2
    full = full.reshape((ring, 2) + full.shape[1:])
    terms = [lax.dynamic_index_in_dim(full, (me - dq + ring) % ring, 0, False) for dq in range(ring)]
    return ring_sum(terms, q_shift, each)


def swap_halves(value):
    bit = lax.axis_index("shard") % 2
    own = lax.dynamic_index_in_dim(value, bit, 0, False)
    other = lax.dynamic_index_in_dim(value, 1 - bit, 0, False)
    return own.astype(f32) + half_swap(other.astype(bf16)).astype(f32)


def attn_parts(q_ref, r_ref, p_ref, k_ref, block, scale):
    size = (block + 1) * BLOCK
    at = pl.ds(block * BLOCK, BLOCK)
    query = q_ref[at, :]
    rope = r_ref[0, at, :]
    keys = p_ref[0:size, 0:DN]
    values = p_ref[0:size, DN : DN + DV]
    key_rope = k_ref[0:size, :]
    scores = (mm_nt(query, keys) + mm_nt(rope, key_rope)) * scale
    weights = jnp.exp(scores - jnp.max(scores, axis=-1, keepdims=True))
    probs = weights / jnp.sum(weights, axis=-1, keepdims=True)
    return query, rope, keys, values, key_rope, probs, size, at


def attn_fwd_kernel(scale, q_ref, r_ref, p_ref, k_ref, o_ref):
    for block in range(q_ref.shape[0] // BLOCK):
        _, _, _, values, _, probs, _, at = attn_parts(q_ref, r_ref, p_ref, k_ref, block, scale)
        o_ref[at, :] = mm(probs.astype(bf16), values).astype(bf16)


def attn_bwd_kernel(scale, q_ref, r_ref, p_ref, k_ref, g_ref, dq_ref, dr_ref, dp_ref, dk_ref, sum_ref):
    @pl.when(pl.program_id(0) == 0)
    def _():
        dk_ref[...] = jnp.zeros_like(dk_ref)

    sum_ref[...] = jnp.zeros_like(sum_ref)
    for block in range(q_ref.shape[0] // BLOCK):
        query, rope, keys, values, key_rope, probs, size, at = attn_parts(
            q_ref, r_ref, p_ref, k_ref, block, scale
        )
        grad = g_ref[at, :]
        low = probs.astype(bf16)
        d_probs = mm_nt(grad, values)
        d_scores = probs * (d_probs - jnp.sum(probs * d_probs, axis=-1, keepdims=True))
        d_scores = d_scores.astype(bf16)
        dq_ref[at, :] = (mm(d_scores, keys) * scale).astype(bf16)
        dr_ref[0, at, :] = mm(d_scores, key_rope) * scale
        sum_ref[0:size, 0:DN] += mm_tn(d_scores, query) * scale
        sum_ref[0:size, DN : DN + DV] += mm_tn(low, grad)
        dk_ref[0:size, :] += mm_tn(d_scores, rope) * scale
    dp_ref[...] = sum_ref[...].astype(bf16)


def attn_specs(seq):
    return [
        pl.BlockSpec((seq, DN), lambda i: (0, i)),
        pl.BlockSpec((1, seq, DR), lambda i: (i, 0, 0)),
        pl.BlockSpec((seq, DN + DV), lambda i: (0, i)),
        pl.BlockSpec((seq, DR), lambda i: (0, 0)),
    ]


def attend(query, rope, pairs, key_rope, scale):
    seq = query.shape[0]
    heads = rope.shape[0]
    return pl.pallas_call(
        functools.partial(attn_fwd_kernel, scale),
        grid=(heads,),
        in_specs=attn_specs(seq),
        out_specs=pl.BlockSpec((seq, DV), lambda i: (0, i)),
        out_shape=jax.ShapeDtypeStruct((seq, heads * DV), bf16),
        compiler_params=pltpu.CompilerParams(vmem_limit_bytes=40 * 1024 * 1024),
        name="attend",
    )(query, rope, pairs, key_rope)


def attend_back(query, rope, pairs, key_rope, grad, scale):
    seq = query.shape[0]
    heads = rope.shape[0]
    return pl.pallas_call(
        functools.partial(attn_bwd_kernel, scale),
        grid=(heads,),
        in_specs=attn_specs(seq) + [pl.BlockSpec((seq, DV), lambda i: (0, i))],
        out_specs=[
            pl.BlockSpec((seq, DN), lambda i: (0, i)),
            pl.BlockSpec((1, seq, DR), lambda i: (i, 0, 0)),
            pl.BlockSpec((seq, DN + DV), lambda i: (0, i)),
            pl.BlockSpec((seq, DR), lambda i: (0, 0)),
        ],
        out_shape=[
            jax.ShapeDtypeStruct((seq, heads * DN), bf16),
            jax.ShapeDtypeStruct((heads, seq, DR), f32),
            jax.ShapeDtypeStruct((seq, heads * (DN + DV)), bf16),
            jax.ShapeDtypeStruct((seq, DR), f32),
        ],
        scratch_shapes=[pltpu.VMEM((seq, DN + DV), f32)],
        compiler_params=pltpu.CompilerParams(vmem_limit_bytes=40 * 1024 * 1024),
        name="attend_back",
    )(query, rope, pairs, key_rope, grad)


def pick_of(info, tri, expert, experts, capacity):
    lanes = lax.broadcasted_iota(jnp.int32, (8, info.shape[1]), 1)
    mine = ((lanes == expert) | (lanes == experts + expert)).astype(f32).astype(bf16)
    weights = mm_nt(mine, info)[0:1, :]
    chosen = weights >= 0.0
    slot = mm(jnp.broadcast_to(chosen.astype(f32).astype(bf16), (8, info.shape[0])), tri)[0:1, :]
    place = lax.broadcasted_iota(jnp.int32, (capacity, info.shape[0]), 0).astype(f32) + 1.0
    pick = chosen & (slot == place)
    weight_row = jnp.sum(jnp.where(pick, weights, 0.0), axis=-1, keepdims=True)
    return pick.astype(f32).astype(bf16), weight_row


def triangle(rows):
    first = lax.broadcasted_iota(jnp.int32, (rows, rows), 0)
    second = lax.broadcasted_iota(jnp.int32, (rows, rows), 1)
    return (first <= second).astype(f32).astype(bf16)


def start_copies(sources, targets, sems, first):
    copies = [
        pltpu.make_async_copy(source, target, sems.at[first + i])
        for i, (source, target) in enumerate(zip(sources, targets))
    ]
    for item in copies:
        item.start()
    return copies


def wait_all(copies):
    for item in copies:
        item.wait()


def taker(refs):
    refs = list(refs)

    def take(count):
        found = refs[:count]
        del refs[:count]
        return found

    return take


WEIGHT_ORDER = (0, 2, 4, 1, 3, 5)


def halves_of(refs, other):
    return [ref for i in range(3) for ref in (refs[i], refs[3].at[other, i])]


def moe_fwd_kernel(dims, expert_ref, *refs):
    index, blocks, rows, width, experts, capacity, aliased = dims
    take = taker(refs)
    block_refs = take(blocks)
    weight_refs = halves_of(take(4), expert_ref[1])
    shared_refs = take(3)
    take(aliased)
    outs = take(blocks)
    keep_refs = take(6)
    flat, out, taken, gates, ups, scaled, shared_gates, shared_ups, made = take(9)
    weights = take(6)
    shared = take(3)
    (sems,) = take(1)
    picked = blocks * capacity
    here = pl.ds(index * picked, picked)
    tokens = pl.ds(index * blocks * rows, blocks * rows)
    spans = [pl.ds(b * rows, rows) for b in range(blocks)]
    arriving = start_copies(block_refs, [flat.at[span, :] for span in spans], sems, 0)
    moving = start_copies(
        [weight_refs[i] for i in WEIGHT_ORDER], [weights[i] for i in WEIGHT_ORDER], sems, blocks
    )
    moving = dict(zip(WEIGHT_ORDER, moving))
    rest = start_copies(shared_refs, shared, sems, blocks + 6)
    expert = expert_ref[0]
    tri = triangle(rows)
    picks = []
    weight_rows = []
    for b in range(blocks):
        arriving[b].wait()
        pick, weight_row = pick_of(flat[spans[b], width:], tri, expert, experts, capacity)
        picks.append(pick)
        weight_rows.append(weight_row)
        taken[pl.ds(b * capacity, capacity), :] = mm(pick, flat[spans[b], 0:width]).astype(bf16)
    leaving = start_copies([taken], [keep_refs[0].at[here, :]], sems, blocks + 9)
    weight_row = jnp.concatenate(weight_rows, 0)
    for side in range(2):
        moving[side].wait()
        gate = mm_nt(taken[...], weights[side][...])
        gates[side] = gate.astype(bf16)
        act = gate * jax.nn.sigmoid(gate) * weight_row
        moving[2 + side].wait()
        up = mm_nt(taken[...], weights[2 + side][...])
        ups[side] = up.astype(bf16)
        scaled[side] = (act * up).astype(bf16)
        moving[4 + side].wait()
        if side:
            made[...] += mm(scaled[side], weights[4 + side][...])
        else:
            made[...] = mm(scaled[side], weights[4 + side][...])
    leaving += start_copies(
        [gates, ups, scaled], [ref.at[:, here, :] for ref in keep_refs[1:4]], sems, blocks + 10
    )
    wait_all(rest)
    gate = mm_nt(flat[:, 0:width], shared[0][...])
    up = mm_nt(flat[:, 0:width], shared[1][...])
    shared_gates[...] = gate
    shared_ups[...] = up
    leaving += start_copies(
        [shared_gates, shared_ups], [ref.at[tokens, :] for ref in keep_refs[4:6]], sems, blocks + 13
    )
    hidden = (gate * jax.nn.sigmoid(gate) * up).astype(bf16)
    for b in range(blocks):
        rows_of = made[pl.ds(b * capacity, capacity), :].astype(bf16)
        out[spans[b], :] = (
            mm_tn(picks[b], rows_of) + mm(hidden[b * rows : (b + 1) * rows, :], shared[2][...])
        ).astype(bf16)
        leaving += start_copies([out.at[spans[b], :]], [outs[b]], sems, blocks + 15 + b)
    wait_all(leaving)


def moe_bwd_kernel(dims, expert_ref, *refs):
    index, blocks, rows, width, experts, capacity, aliased = dims
    take = taker(refs)
    error_refs = take(blocks)
    block_refs = take(blocks)
    weight_refs = halves_of(take(4), expert_ref[1])
    shared_refs = take(3)
    kept_refs = take(4)
    take(aliased)
    outs = take(blocks)
    sum_refs = take(3)
    keep_refs = take(3)
    errors, flat, taken, gates, ups, d_gates, d_ups, shared_gates, shared_ups, made = take(10)
    sums = take(3)
    weights = take(6)
    shared = take(3)
    (sems,) = take(1)
    picked = blocks * capacity
    here = pl.ds(index * picked, picked)
    tokens = pl.ds(index * blocks * rows, blocks * rows)
    spans = [pl.ds(b * rows, rows) for b in range(blocks)]
    arriving = start_copies(error_refs, [errors.at[span, 0:width] for span in spans], sems, 0)
    inputs = start_copies(block_refs, [flat.at[span, :] for span in spans], sems, blocks)
    first = 2 * blocks
    order = (4, 0, 2, 5, 1, 3)
    kept = start_copies(
        [ref.at[:, here, :] for ref in kept_refs[0:2]], [gates, ups], sems, first
    )
    moving = start_copies(
        [weight_refs[i] for i in order], [weights[i] for i in order], sems, first + 2
    )
    moving = dict(zip(order, moving))
    kept_shared = start_copies(
        [ref.at[tokens, :] for ref in kept_refs[2:4]], [shared_gates, shared_ups], sems, first + 8
    )
    rest = start_copies(shared_refs, shared, sems, first + 10)
    first = first + 13
    expert = expert_ref[0]
    tri = triangle(rows)
    picks = []
    weight_rows = []
    for b in range(blocks):
        inputs[b].wait()
        arriving[b].wait()
        pick, weight_row = pick_of(flat[spans[b], width:], tri, expert, experts, capacity)
        picks.append(pick)
        weight_rows.append(weight_row)
        taken[pl.ds(b * capacity, capacity), :] = mm(pick, errors[spans[b], 0:width]).astype(bf16)
    leaving = start_copies([taken], [keep_refs[0].at[here, :]], sems, first)
    weight_row = jnp.concatenate(weight_rows, 0)
    wait_all(kept)
    d_weight = 0.0
    for side in range(2):
        moving[4 + side].wait()
        d_plain = mm_nt(taken[...], weights[4 + side][...])
        gate = gates[side].astype(f32)
        up = ups[side].astype(f32)
        act, slope = silu_parts(gate)
        d_weight = d_weight + jnp.sum(act * up * d_plain, axis=-1, keepdims=True)
        d_hidden = d_plain * weight_row
        d_gates[side] = (d_hidden * up * slope).astype(bf16)
        d_ups[side] = (d_hidden * act).astype(bf16)
        moving[side].wait()
        moving[2 + side].wait()
        back = mm(d_gates[side], weights[side][...]) + mm(d_ups[side], weights[2 + side][...])
        if side:
            made[...] += back
        else:
            made[...] = back
    leaving += start_copies(
        [d_gates, d_ups], [ref.at[:, here, :] for ref in keep_refs[1:3]], sems, first + 1
    )
    wait_all(rest)
    wait_all(kept_shared)
    act, slope = silu_parts(shared_gates[...])
    shared_up = shared_ups[...]
    d_hidden = mm_nt(errors[:, 0:width], shared[2][...])
    d_gate = (d_hidden * shared_up * slope).astype(bf16)
    d_up = (d_hidden * act).astype(bf16)
    sums[0][...] = mm_tn(d_gate, flat[:, 0:width])
    sums[1][...] = mm_tn(d_up, flat[:, 0:width])
    sums[2][...] = mm_tn((act * shared_up).astype(bf16), errors[:, 0:width])
    leaving += start_copies(sums, sum_refs, sems, first + 3)
    info_cols = flat.shape[1] - width
    lanes = lax.broadcasted_iota(jnp.int32, (capacity, info_cols), 1)
    for b in range(blocks):
        rows_of = made[pl.ds(b * capacity, capacity), :].astype(bf16)
        span = slice(b * rows, (b + 1) * rows)
        errors[spans[b], 0:width] = (
            mm_tn(picks[b], rows_of)
            + mm(d_gate[span, :], shared[0][...])
            + mm(d_up[span, :], shared[1][...])
        ).astype(bf16)
        column = d_weight[b * capacity : (b + 1) * capacity, :]
        high = column.astype(bf16).astype(f32)
        found = jnp.where(lanes == expert, high, 0.0)
        found = jnp.where(lanes == experts + expert, column - high, found)
        errors[spans[b], width:] = mm_tn(picks[b], found.astype(bf16)).astype(bf16)
        leaving += start_copies([errors.at[spans[b], :]], [outs[b]], sems, first + 6 + b)
    wait_all(leaving)


def moe_call(kernel, dims, expert, groups, before, out_blocks, out_plain, out_kept, scratch, copies, cost, name):
    operands = [item for group in groups for item in group] + list(before)
    anywhere = pl.BlockSpec(memory_space=pl.ANY)
    shapes = out_blocks + out_plain + out_kept
    first = 1 + len(operands) - len(before)
    return pl.pallas_call(
        functools.partial(kernel, dims + (len(before),)),
        in_specs=[pl.BlockSpec(memory_space=pltpu.SMEM)] + [anywhere] * len(operands),
        out_specs=[anywhere] * len(shapes),
        out_shape=shapes,
        scratch_shapes=scratch + [pltpu.SemaphoreType.DMA((copies,))],
        input_output_aliases={
            first + i: len(out_blocks) + len(out_plain) + i for i in range(len(before))
        },
        compiler_params=pltpu.CompilerParams(vmem_limit_bytes=60 * 1024 * 1024),
        cost_estimate=cost,
        name=name,
    )(expert, *operands)


def moe_fwd(index, chunks, expert, experts, capacity, blocks, weights, shared, kept):
    count = len(blocks)
    rows = blocks[0].shape[0]
    half, width = weights[0].shape
    hidden = shared[0].shape[0]
    taken = count * capacity
    tokens = count * rows
    shape = jax.ShapeDtypeStruct
    result = moe_call(
        moe_fwd_kernel,
        (index, count, rows, width, experts, capacity),
        expert,
        (blocks, weights, shared),
        [] if kept is None else kept,
        [shape((rows, width), bf16)] * count,
        [],
        [shape((chunks * taken, width), bf16)]
        + [shape((2, chunks * taken, half), bf16)] * 3
        + [shape((chunks * tokens, hidden), f32)] * 2,
        [
            pltpu.VMEM((tokens, blocks[0].shape[1]), bf16),
            pltpu.VMEM((tokens, width), bf16),
            pltpu.VMEM((taken, width), bf16),
            pltpu.VMEM((2, taken, half), bf16),
            pltpu.VMEM((2, taken, half), bf16),
            pltpu.VMEM((2, taken, half), bf16),
            pltpu.VMEM((tokens, hidden), f32),
            pltpu.VMEM((tokens, hidden), f32),
            pltpu.VMEM((taken, width), f32),
        ]
        + [pltpu.VMEM((half, width), bf16)] * 6
        + [pltpu.VMEM((hidden, width), bf16)] * 3,
        2 * count + 15,
        pl.CostEstimate(flops=0, bytes_accessed=0, transcendentals=0),
        "moe_fwd",
    )
    return list(result[:count]), list(result[count:])


def moe_bwd(index, chunks, expert, experts, capacity, errors, blocks, weights, shared, kept, before):
    count = len(blocks)
    rows = blocks[0].shape[0]
    half, width = weights[0].shape
    hidden = shared[0].shape[0]
    taken = count * capacity
    tokens = count * rows
    shape = jax.ShapeDtypeStruct
    result = moe_call(
        moe_bwd_kernel,
        (index, count, rows, width, experts, capacity),
        expert,
        (errors, blocks, weights, shared, kept),
        [] if before is None else before,
        [shape(blocks[0].shape, bf16)] * count,
        [shape((hidden, width), f32)] * 3,
        [shape((chunks * taken, width), bf16)] + [shape((2, chunks * taken, half), bf16)] * 2,
        [
            pltpu.VMEM((tokens, blocks[0].shape[1]), bf16),
            pltpu.VMEM((tokens, blocks[0].shape[1]), bf16),
            pltpu.VMEM((taken, width), bf16),
            pltpu.VMEM((2, taken, half), bf16),
            pltpu.VMEM((2, taken, half), bf16),
            pltpu.VMEM((2, taken, half), bf16),
            pltpu.VMEM((2, taken, half), bf16),
            pltpu.VMEM((tokens, hidden), f32),
            pltpu.VMEM((tokens, hidden), f32),
            pltpu.VMEM((taken, width), f32),
        ]
        + [pltpu.VMEM((hidden, width), f32)] * 3
        + [pltpu.VMEM((half, width), bf16)] * 6
        + [pltpu.VMEM((hidden, width), bf16)] * 3,
        3 * count + 19,
        pl.CostEstimate(flops=0, bytes_accessed=0, transcendentals=0),
        "moe_bwd",
    )
    return list(result[:count]), list(result[count : count + 3]), list(result[count + 3 :])


def on_device(
    tokens,
    target,
    routes,
    attn_gain,
    w_query,
    w_latent_in,
    latent_gain,
    w_latent_out,
    w_attn_out,
    ffn_gain,
    w_router,
    shared_gate,
    shared_up,
    shared_down,
    expert_gate,
    expert_up,
    expert_down,
):
    rows = tokens.shape[1]
    width = tokens.shape[2]
    ctx_count = lax.axis_size("ctx")
    shard_count = lax.axis_size("shard")
    chips = ctx_count // 2
    ring = shard_count // 2
    experts = ctx_count * ring
    capacity = max(2, (rows * TOP * 4 + experts * 3 - 1) // (experts * 3))
    seq_len = rows * ctx_count
    own_heads = H // ctx_count
    scale = (DN + DR) ** (-0.5)
    ctx = lax.axis_index("ctx")
    shard = lax.axis_index("shard")
    expert = ctx * ring + shard // 2
    devices = ctx_count * shard_count
    piece = width // devices

    depth = w_query.shape[0]
    lat_rows = latent_gain.shape[0]
    part = depth // ctx_count
    lat_part = lat_rows // ctx_count
    half_bit = shard % 2
    small = jnp.concatenate(
        [
            w_latent_in,
            attn_gain[:, None],
            ffn_gain[:, None],
            jnp.pad(latent_gain.reshape(ctx_count, lat_part), ((0, 0), (0, part - lat_part)))
            .reshape(depth, 1),
            w_router,
        ],
        1,
    )
    small = jnp.pad(small, ((0, 0), (0, -small.shape[1] % LANES)))
    small = lax.dynamic_slice_in_dim(small, ctx * part, part, 0)
    own_query = lax.dynamic_slice_in_dim(
        w_query, ctx * own_heads * (DN + DR), own_heads * (DN + DR), 1
    ).reshape(depth, own_heads, DN + DR)
    plain_cols = own_heads * DN
    rope_cols = own_heads * DR
    packed = jnp.concatenate(
        [
            own_query[..., :DN].reshape(depth, plain_cols),
            own_query[..., DN:].reshape(depth, rope_cols),
        ],
        1,
    )
    own_pairs = own_heads * (DN + DV)
    up_piece = lax.dynamic_slice_in_dim(w_latent_out, ctx * own_pairs, own_pairs, 1)
    packed = jnp.concatenate([packed, up_piece.reshape(depth, -1)], 1)
    packed_pair = both_of(packed, half_swap(packed), half_bit)
    out_piece = 0.0
    for j in range(ctx_count):
        moves = []
        for t in range(shard_count):
            to = t * ctx_count + j
            base = (to // shard_count) * shard_count
            moves.append((base + t, to))
        out_piece = out_piece + lax.ppermute(
            w_attn_out[j * piece : (j + 1) * piece], ("ctx", "shard"), moves
        )
    out_pair = both_of(out_piece, half_swap(out_piece), half_bit)

    slice_rows = shared_down.shape[0] // ctx_count
    down_own = lax.dynamic_slice_in_dim(shared_down, ctx * slice_rows, slice_rows, 0)
    down_other = half_swap(down_own)
    both = jnp.stack([shared_gate, shared_up], 0).reshape(
        2, depth, ring, 2, ctx_count, slice_rows
    )
    both = lax.dynamic_index_in_dim(both, ctx, 4, False).transpose(2, 3, 0, 4, 1)
    both = jnp.stack([both, both[:, ::-1]], 1)
    both = both.reshape(shard_count, 4 * slice_rows, depth)
    both = lax.all_to_all(both, "shard", split_axis=0, concat_axis=0, tiled=True)
    both = both.transpose(1, 0, 2).reshape(2, 2, slice_rows, width)
    shared_all = [both[:, i].reshape(2 * slice_rows, width) for i in range(2)]
    shared_all.append(jnp.concatenate([down_own, down_other], 0))

    small = gather_shard_from(both_of(small, half_swap(small), half_bit))
    small = after(small, both, down_other)
    small = gather_ctx_rows(small).reshape(ctx_count, shard_count, part, -1)
    latent_cols = LAT + DR
    small_gains = small[..., latent_cols : latent_cols + 3].transpose(3, 1, 0, 2)
    gain_attn = small_gains[0].reshape(width).astype(f32)
    gain_ffn = small_gains[1].reshape(width).astype(f32)
    gain_latent = small_gains[2, :, :, :lat_part].reshape(LAT).astype(f32)
    small = small.transpose(1, 0, 2, 3).reshape(width, -1)
    latent_down = small[:, :latent_cols]
    router_proj = small[:, latent_cols + 3 : latent_cols + 3 + experts]

    own_half = [expert_gate[0].T, expert_up[0].T, expert_down[0]]
    weights_all = own_half + [both_halves(jnp.stack(own_half, 0))]

    gathered = gather_shard_from(packed_pair)
    plain_proj = gathered[:, :plain_cols]
    rope_proj = gathered[:, plain_cols : plain_cols + rope_cols]
    packed = gathered[:, : plain_cols + rope_cols]
    latent_up = gathered[:, plain_cols + rope_cols :].reshape(LAT, own_pairs)
    out_proj = gather_shard_from(after(out_pair, gathered))

    source = tokens[0].astype(f32)
    factor_attn = inverse_root(source)
    all_source = gather_ctx_rows(tokens[0]).astype(f32)
    attn_in = (all_source * inverse_root(all_source) * gain_attn).astype(bf16)
    cosine, sine = tables(jnp.arange(seq_len), DR)
    query = mm(attn_in, plain_proj).astype(bf16)
    query_rope = jnp.einsum(
        "td,dhk->htk",
        attn_in,
        rope_proj.reshape(width, own_heads, DR),
        preferred_element_type=f32,
    )
    query_rope = rotate(query_rope, cosine, sine).astype(bf16)
    latent_raw = mm(attn_in, latent_down)
    latent_part = latent_raw[:, :LAT]
    latent = (latent_part * inverse_root(latent_part) * gain_latent).astype(bf16)
    key_rope = rotate(latent_raw[:, LAT:], cosine, sine).astype(bf16)
    pairs = mm(latent, latent_up).astype(bf16)
    heads = attend(query, query_rope, pairs, key_rope, scale)
    middle = source + scatter_ctx(mm(heads, out_proj).astype(bf16))

    factor_ffn = inverse_root(middle)
    ffn_in = (middle * factor_ffn * gain_ffn).astype(bf16)
    router = jax.nn.softmax(mm(ffn_in, router_proj), axis=-1)
    chosen_any = jnp.any(
        routes[0][:, :, None] == jnp.arange(experts, dtype=jnp.int32)[None, None, :], axis=1
    )
    weight = jnp.where(chosen_any, router, -1.0)
    weight_high = weight.astype(bf16)
    weight_low = (weight - weight_high.astype(f32)).astype(bf16)
    info = jnp.concatenate(
        [
            weight_high,
            weight_low,
            jnp.zeros((rows, max(0, LANES - 2 * experts)), bf16),
        ],
        1,
    )
    info_cols = info.shape[1]

    expert_at = jnp.stack([expert, 1 - half_bit]).astype(jnp.int32)

    def through(block, work, last=None, each=None):
        gate = expert_at
        sums = []
        done = []
        for step in range(ring):
            if step:
                block = q_shift(block)
            if step > 1:
                block = after(block, done[-2])
            found = work(step, [item for pair in gather_x(block) for item in pair], gate)
            done.append(found[0])
            pairs = [
                found[2 * i].astype(f32) + core_swap(found[2 * i + 1]).astype(f32)
                for i in range(chips)
            ]
            waits = [pairs[-1]] + (sums[-1:] if step > 1 else [])
            if step == ring - 1 and last is not None:
                pairs[0] = last(pairs[0])
            sums.append(ring_sum(pairs, x_shift))
            gate = after(expert_at, waits)
        return ring_sum(sums, q_shift, each)

    in_chunks = []
    kept = None

    def forward(index, chunk, gate):
        nonlocal kept
        in_chunks.append(chunk)
        out, kept = moe_fwd(
            index, ring, gate, experts, capacity, chunk, weights_all, shared_all, kept
        )
        return out

    final = middle + through(jnp.concatenate([ffn_in, info], 1), forward)
    error = final - target[0].astype(f32)
    loss_part = jnp.sum(error * error)

    d_shared = []
    d_kept = None

    def backward(index, chunk, gate):
        nonlocal d_kept
        out, part, d_kept = moe_bwd(
            index,
            ring,
            gate,
            experts,
            capacity,
            chunk,
            in_chunks[index],
            weights_all,
            shared_all,
            [kept[1], kept[2], kept[4], kept[5]],
            d_kept,
        )
        d_shared.append(part)
        return out

    def half_grads(half):
        taken, scaled = kept[0], kept[3]
        d_taken, d_gates, d_ups = d_kept
        return (mm_tn(d_gates[half], taken), mm_tn(d_ups[half], taken), mm_tn(scaled[half], d_taken))

    block = error.astype(bf16)
    terms = []
    for step in range(ring):
        if step:
            block = q_shift(block)
        found = backward(step, [item for pair in gather_x(block) for item in pair], expert_at)
        pairs_of = [[found[2 * i], found[2 * i + 1]] for i in range(chips)]
        terms.append(scatter_x(pairs_of))
    d_all = ring_sum(terms, q_shift)
    for_other = [item.astype(bf16) for item in half_grads(1)]
    d_slices = jnp.stack([sum(item[i] for item in d_shared) for i in range(3)], 0)
    d_slices = d_slices.reshape(3, 2, slice_rows, width)
    found = half_swap(d_slices[:, 1].astype(bf16))
    d_slices = (d_slices[:, 0] + found.astype(f32)).astype(bf16)
    from_other = [
        both_halves(for_other[0]),
        both_halves(after(jnp.stack(for_other[1:], 0), found)),
    ]

    d_ffn = d_all[:, :width]
    d_info = d_all[:, width:]
    d_router = d_info[:, :experts] + d_info[:, experts : 2 * experts]
    d_router = jnp.where(chosen_any, d_router, 0.0)

    d_logits = (router * (d_router - jnp.sum(router * d_router, axis=-1, keepdims=True))).astype(
        bf16
    )
    d_router_proj = mm_tn(ffn_in, d_logits)
    d_ffn = d_ffn + mm_nt(d_logits, router_proj)
    d_middle_norm, d_gain_ffn = norm_back(middle, factor_ffn, gain_ffn, d_ffn)
    d_middle = error + d_middle_norm

    d_branch = gather_ctx_rows(d_middle.astype(bf16))
    d_out_proj = mm_tn(heads, d_branch).astype(bf16)
    d_heads = mm_nt(d_branch, out_proj).astype(bf16)
    d_heads = after(d_heads, d_out_proj, from_other[0])
    d_query, d_rope, d_pairs, d_key_rope = attend_back(
        query, query_rope, pairs, key_rope, d_heads, scale
    )
    d_latent_sum = jnp.concatenate([mm_nt(d_pairs, latent_up), d_key_rope], 1).astype(bf16)
    d_latent_cores = sum_cores(d_latent_sum)
    d_latent = sum_chips(d_latent_cores)
    d_rope = rotate_back(d_rope, cosine, sine).astype(bf16)
    d_rope = d_rope.transpose(1, 0, 2).reshape(seq_len, rope_cols)
    d_query = after(jnp.concatenate([d_query, d_rope], 1), d_latent_sum)
    d_latent_part, _ = norm_back(
        latent_part, inverse_root(latent_part), gain_latent, d_latent[:, :LAT]
    )
    d_latent_raw = jnp.concatenate(
        [d_latent_part, rotate_back(d_latent[:, LAT:], cosine, sine)], -1
    ).astype(bf16)
    first = ctx * rows
    own_latent = lax.dynamic_slice_in_dim(latent_part, first, rows, 0)
    own_grads = lax.dynamic_slice_in_dim(d_latent, first, rows, 0)[:, :LAT]
    d_gain_latent = jnp.sum(own_grads * own_latent * inverse_root(own_latent), axis=0)
    latent_cols = (LAT + DR) // ctx_count
    d_latent_all = lax.dynamic_slice_in_dim(
        d_latent_raw, ctx * latent_cols, latent_cols, 1
    )
    d_packed = mm_tn(attn_in, d_query).astype(bf16)
    d_attn_in = scatter_ctx(
        mm_nt(after(d_query, d_packed, d_latent_cores), packed).astype(bf16)
    ) + mm_nt(lax.dynamic_slice_in_dim(d_latent_raw, first, rows, 0), latent_down)
    d_latent_up = mm_tn(latent, d_pairs)
    d_source_norm, d_gain_attn = norm_back(source, factor_attn, gain_attn, d_attn_in)
    token_grad = d_middle + d_source_norm

    def by_rows(value):
        cols = value.shape[1]
        return value.astype(bf16).reshape(ctx_count, shard_count, -1, cols).transpose(1, 0, 2, 3)

    early = jnp.concatenate(
        [
            d_out_proj.reshape(shard_count, -1, LANES),
            by_rows(d_packed).reshape(shard_count, -1, LANES),
            by_rows(d_latent_up).reshape(shard_count, -1, LANES),
        ],
        1,
    )
    from_other = [
        lax.dynamic_index_in_dim(after(item, late), 1 - half_bit, 0, False)
        for item, late in zip(from_other, (d_packed, d_packed))
    ]
    from_other = [from_other[0], from_other[1][0], from_other[1][1]]
    d_expert = [item + other.astype(f32) for item, other in zip(half_grads(0), from_other)]

    d_both = d_slices[:2].reshape(2, slice_rows, devices, piece)
    d_both = lax.all_to_all(
        d_both.transpose(2, 0, 1, 3).reshape(devices, 2 * slice_rows, piece),
        ("ctx", "shard"),
        split_axis=0,
        concat_axis=0,
        tiled=True,
    )
    sum_early = ring_shard(
        early, lambda place, total: total if place else after(total, d_both)
    )
    d_latent_in = mm_tn(attn_in, d_latent_all).astype(bf16)
    latent_terms = d_latent_in.reshape(ctx_count, ring, 2, piece, latent_cols)
    sum_latents = ring_sum(
        [
            lax.dynamic_index_in_dim(latent_terms, (shard // 2 - dq + ring) % ring, 1, False)
            for dq in range(ring)
        ],
        q_shift,
    )
    sum_latents = swap_halves(sum_latents.transpose(1, 0, 2, 3)).astype(bf16)
    flat = swap_halves(sum_early).astype(bf16)
    out_rows = d_out_proj.size // (shard_count * LANES)
    packed_rows = d_packed.size // (shard_count * LANES)
    g_attn_out = flat[:out_rows].astype(f32).reshape(piece, width)
    flat = jnp.concatenate(
        [
            flat[out_rows : out_rows + packed_rows].reshape(ctx_count, -1, LANES),
            flat[out_rows + packed_rows :].reshape(ctx_count, -1, LANES),
            sum_latents.reshape(ctx_count, -1, LANES),
        ],
        1,
    )
    packed_rows = packed_rows // ctx_count
    up_rows = d_latent_up.size // (shard_count * ctx_count * LANES)
    flat = lax.all_to_all(flat, "ctx", split_axis=0, concat_axis=0, tiled=True).astype(f32)
    g_packed = flat[:, :packed_rows].reshape(ctx_count, piece, -1)
    g_plain = g_packed[..., :plain_cols].reshape(ctx_count, piece, own_heads, DN)
    g_rope = g_packed[..., plain_cols:].reshape(ctx_count, piece, own_heads, DR)
    g_query = jnp.concatenate([g_plain, g_rope], -1).transpose(1, 0, 2, 3).reshape(piece, -1)
    g_latent_out = flat[:, packed_rows : packed_rows + up_rows]
    g_latent_out = g_latent_out.reshape(ctx_count, LAT // devices, -1)
    g_latent_out = g_latent_out.transpose(1, 0, 2).reshape(LAT // devices, -1)
    g_latent_in = flat[:, packed_rows + up_rows :].reshape(ctx_count, piece, latent_cols)
    g_latent_in = g_latent_in.transpose(1, 0, 2).reshape(piece, -1)

    d_expert = [d_expert[0].T, d_expert[1].T, d_expert[2]]

    moves = []
    for a in range(ctx_count):
        for b in range(shard_count):
            moves.append((a * shard_count + b, b * ctx_count + a))
    g_down = lax.ppermute(after(d_slices[2], d_packed), ("ctx", "shard"), moves)
    g_down = after(g_down, sum_early).astype(f32)
    d_both = after(d_both, d_attn_in).reshape(ctx_count, shard_count, 2, slice_rows, piece)
    d_both = d_both.transpose(2, 4, 1, 0, 3).reshape(2, piece, -1).astype(f32)
    g_gate = d_both[0]
    g_up = d_both[1]

    small_sums = jnp.concatenate(
        [
            d_gain_ffn.reshape(devices, piece),
            d_router_proj.reshape(devices, piece * experts),
            d_gain_attn.reshape(devices, piece),
            d_gain_latent.reshape(devices, -1),
            jnp.broadcast_to(loss_part, (devices, 1)),
        ],
        1,
    )
    small_sums = all_sum(small_sums)
    g_ffn = small_sums[:piece]
    at = piece + piece * experts
    g_router = small_sums[piece:at].reshape(piece, experts)
    g_attn = small_sums[at : at + piece]
    g_latent = small_sums[at + piece : -1]
    loss = small_sums[-1] / (rows * devices * width)

    return (
        final.astype(bf16)[None],
        loss,
        token_grad[None],
        g_attn,
        g_query,
        g_latent_in,
        g_latent,
        g_latent_out,
        g_attn_out,
        g_ffn,
        g_router,
        g_gate,
        g_up,
        g_down,
        d_expert[0][None],
        d_expert[1][None],
        d_expert[2][None],
    )


def solution(mesh):
    in_specs = (
        P("shard", "ctx", None),
        P("shard", "ctx", None),
        P("shard", "ctx", None),
        P("shard"),
        P("shard", None),
        P("shard", None),
        P("shard"),
        P("shard", None),
        P("shard", None),
        P("shard"),
        P("shard", None),
        P("shard", None),
        P("shard", None),
        P("shard", None),
        P(("ctx", "shard"), None, None),
        P(("ctx", "shard"), None, None),
        P(("ctx", "shard"), None, None),
    )
    out_specs = (
        P("shard", "ctx", None),
        P(),
        P("shard", "ctx", None),
        P(("ctx", "shard")),
        P(("ctx", "shard"), None),
        P(("ctx", "shard"), None),
        P(("ctx", "shard")),
        P(("ctx", "shard"), None),
        P(("ctx", "shard"), None),
        P(("ctx", "shard")),
        P(("ctx", "shard"), None),
        P(("ctx", "shard"), None),
        P(("ctx", "shard"), None),
        P(("ctx", "shard"), None),
        P(("ctx", "shard"), None, None),
        P(("ctx", "shard"), None, None),
        P(("ctx", "shard"), None, None),
    )
    return jax.shard_map(
        on_device, mesh=mesh, in_specs=in_specs, out_specs=out_specs, check_vma=False
    )
```
